32 devices in a mesh: grp: 2 (over x), wide: 16 (over z, y, core).
Axes of the slice: x: 2, y: 2, z: 4, core: 2. Of those that a mesh axis runs over, the one named last changes fastest.
Arguments:
- query_rows: bfloat16 [2048, 2048], P(('grp', 'wide')), parts along dimension 0, may hold values from -10 to 10
- row_key_value: bfloat16 [2048, 512], P(('grp', 'wide')), parts along dimension 0, may hold values from -6 to 6
- key_value_cache: bfloat16 [65536, 512], P(('grp', 'wide')), parts along dimension 0, may hold values from -5 to 5
- resid: bfloat16 [2048, 2048], P(('grp', 'wide')), parts along dimension 0, may hold values from -12 to 12
- norm_gain: float32 [2048], replicated, may hold values from 0.5 to 1.5
- lengths: int32 [16], P('grp'), parts along dimension 0, may hold values from 1024 to 4096, as said below
- positions: int32 [16, 128], P('grp'), parts along dimension 0, may hold values from 0 to 4095, as said below
- expert_ids: int32 [2048, 8], P(('grp', 'wide')), parts along dimension 0, may hold values from 0 to 15, all different within a row; in each aligned block of 64 rows (0 to 63, 64 to 127, ...) at most 48 rows name the same one
- gate_scores: float32 [2048, 8], P(('grp', 'wide')), parts along dimension 0, may hold values from 0.1 to 1
- w_gate: bfloat16 [16, 2048, 768], P('wide'), may hold values from -0.125 to 0.125
- w_up: bfloat16 [16, 2048, 768], P('wide'), may hold values from -0.125 to 0.125
- w_down: bfloat16 [16, 768, 2048], P('wide'), may hold values from -0.21875 to 0.21875
Outputs:
- out_rows: bfloat16 [2048, 2048], P(('grp', 'wide')), parts along dimension 0
The draws below stay inside these ranges and needn't reach their ends.
There are 2 independent parts, one for each index of `grp`. The reference program is written for one: setup_inputs(seed, part) draws one part's arguments, and reference() takes and returns one part's arrays. A program takes and returns all parts, laid end to end along the dimension named above; an argument that names none is the same for every part. Nothing has to cross between parts.
Inputs may be any that keep to these rules, and one draw needn't show every extreme that they name: `lengths`: one document has length exactly 4096 and another exactly 1024. Within a document the positions are distinct and below its length. `expert_ids`: the 64 rows of one device name each expert at most 48 times, and some expert exactly that often.
All inputs are finite; a program needn't handle non-finite values.
Results may differ from the reference program's by a relative error of at most 0.0095.
Values may be sent and summed in bfloat16 or wider, within the bound.
A program may use at most 128 MiB of HBM per device.

```python
import math
import jax
import jax.numpy as jnp
import numpy as np
from jax import lax

D = 2048
QUERY_HEADS = 32
KEY_VALUE_HEADS = 4
HEAD_SIZE = 64
FF = 768
TOP = 8
HALF_DOC_ROWS = 64
CACHED_POSITIONS = 2048
DOCUMENT_COUNT = 8
MASKED_ROWS = 1024
EXPERTS = 16
MOST = 48
N_WIDE = 16


def doc_layout(key):
    layout_key = jax.random.fold_in(key, 11)
    length_key, full_key, offset_key = jax.random.split(layout_key, 3)
    lengths = jax.random.randint(length_key, (DOCUMENT_COUNT,), CACHED_POSITIONS // 2, 2 * CACHED_POSITIONS + 1)
    full_doc = jax.random.randint(full_key, (), 0, DOCUMENT_COUNT)
    short_doc = (full_doc + 1) % DOCUMENT_COUNT
    doc_range = jnp.arange(DOCUMENT_COUNT)
    lengths = jnp.where(doc_range == full_doc, 2 * CACHED_POSITIONS, lengths)
    lengths = jnp.where(doc_range == short_doc, CACHED_POSITIONS // 2, lengths).astype(jnp.int32)
    stride = lengths // (2 * HALF_DOC_ROWS)
    offsets = jax.random.randint(offset_key, (DOCUMENT_COUNT, 2 * HALF_DOC_ROWS), 0, stride[:, None])
    slot_range = jnp.arange(2 * HALF_DOC_ROWS)
    is_full = (doc_range == full_doc)[:, None]
    offsets = jnp.where(is_full & (slot_range[None, :] == 0), 0, offsets)
    offsets = jnp.where(is_full & (slot_range[None, :] == 2 * HALF_DOC_ROWS - 1), stride[:, None] - 1, offsets)
    positions = slot_range[None, :].astype(jnp.int32) * stride[:, None] + offsets
    return (lengths, positions.astype(jnp.int32))


def draw_lengths(key, part):
    lengths, positions = doc_layout(key)
    return lengths


def draw_positions(key, part):
    lengths, positions = doc_layout(key)
    return positions


def draw_query_rows(key, part):
    subkey = jax.random.fold_in(key, 1)
    array_shape = (DOCUMENT_COUNT, 2 * HALF_DOC_ROWS, QUERY_HEADS * HEAD_SIZE)
    base_draw = jnp.clip(2.5 * jax.random.normal(subkey, array_shape, jnp.float32), -10.0, 10.0)
    return base_draw.reshape(MASKED_ROWS, QUERY_HEADS * HEAD_SIZE).astype(jnp.bfloat16)


def draw_row_key_value(key, part):
    key_draw, value_draw = jax.random.split(jax.random.fold_in(key, 2))
    array_shape = (DOCUMENT_COUNT, 2 * HALF_DOC_ROWS, KEY_VALUE_HEADS * HEAD_SIZE)
    key_portion = jnp.clip(1.6 * jax.random.normal(key_draw, array_shape, jnp.float32), -6.0, 6.0)
    value_portion = jnp.clip(jax.random.normal(value_draw, array_shape, jnp.float32), -5.0, 5.0)
    joined_parts = jnp.concatenate([key_portion, value_portion], axis=-1)
    return joined_parts.reshape(MASKED_ROWS, 2 * KEY_VALUE_HEADS * HEAD_SIZE).astype(jnp.bfloat16)


def draw_key_value_cache(key, part):
    base_key = jax.random.fold_in(jax.random.fold_in(key, 3), 0)
    array_shape = (DOCUMENT_COUNT * 2 * CACHED_POSITIONS, 2 * KEY_VALUE_HEADS * HEAD_SIZE)
    base_draw = jnp.clip(jax.random.normal(base_key, array_shape, jnp.float32), -5.0, 5.0)
    return base_draw.astype(jnp.bfloat16)


def draw_resid(key, part):
    base_key = jax.random.fold_in(jax.random.fold_in(key, 4), 0)
    array_shape = (MASKED_ROWS, D)
    base_draw = jnp.clip(jax.random.normal(base_key, array_shape, jnp.float32), -6.0, 6.0)
    return base_draw.astype(jnp.bfloat16)


def steps_of(rng, shape, cuts, least, high):
    loudness, own = 1.0, jax.random.fold_in(rng, 6)
    for position, blocks in cuts:
        heights = jnp.exp(jax.random.uniform(jax.random.fold_in(own, position), (blocks,), jnp.float32, least / len(cuts), high / len(cuts)))
        loudness = loudness * jnp.repeat(heights, shape[position] // blocks).reshape([-1 if axis == position else 1 for axis in range(len(shape))])
    return loudness


def assign_block(rng, own, number, rows, number_of, top, limit, slope):
    ranking = jax.random.permutation(rng, number_of)
    heavy_load, ordinary = portions_of(number_of, rows * top, limit, slope, True), portions_of(number_of, rows * top, limit, slope, False)
    places = jnp.arange(number_of)

    def named(sizes, offset_by):
        used = int((sizes > 0).sum())
        fixed = max(1, used // 4)
        passed = fixed + (places - fixed + offset_by * (used - fixed)) % max(1, number_of - fixed)
        return jnp.zeros((number_of,), jnp.int32).at[ranking[jnp.where(places < fixed, places, passed)]].set(jnp.asarray(sizes, jnp.int32))

    sizes = jnp.where(number % 4 == 0, named(heavy_load, number // 4), named(ordinary, number - number // 4 - 1))
    mixed = jax.random.permutation(jax.random.fold_in(own, 3), number_of)
    donor, receiver = mixed[0:number_of // 2 * 2:2], mixed[1:number_of // 2 * 2:2]
    room = jnp.minimum(sizes[donor] - 1, limit - sizes[receiver]) // 2
    room = jnp.where((donor == ranking[0]) | (receiver == ranking[0]) | (sizes[receiver] == 0), 0, jnp.maximum(room, 0))
    passed = jax.random.randint(jax.random.fold_in(own, 4), (number_of // 2,), 0, 1 << 20) % (room + 1)
    sizes = sizes.at[donor].add(-passed).at[receiver].add(passed)
    items = jnp.searchsorted(jnp.cumsum(sizes), jnp.arange(rows * top), side="right").astype(jnp.int32)
    table = items.reshape(top, rows).T
    table = table[jax.random.permutation(jax.random.fold_in(own, 1), rows)]
    offset_by = jax.random.randint(jax.random.fold_in(own, 2), (rows, 1), 0, top)
    return jnp.take_along_axis(table, (jnp.arange(top)[None, :] + offset_by) % top, axis=1)


def portions_of(amount, total, most, lean, full):
    portions = [(1 << 20) // math.isqrt(standing ** lean) + 1 for standing in range(1, amount + 1)]
    largest = most if full else min(most, max(-(-total // amount), total * portions[0] // sum(portions)))
    least = 1 if total - largest >= amount - 1 else 0
    given, spare = [largest] + [least] * (amount - 1), total - largest - least * (amount - 1)
    while spare > 0:
        free = [i for i in range(1, amount) if given[i] < largest] or [i for i in range(1, amount) if given[i] < most]
        pool, left = sum([portions[i] for i in free]), spare
        for i in free:
            extra = min(most - given[i], max(1, left * portions[i] // pool), spare)
            given[i] = given[i] + extra
            spare = spare - extra
    return np.array(given)


def gaussian(key, extent, deviation, most, cuts=(), kind=jnp.bfloat16):
    values = deviation * jax.random.normal(key, extent, jnp.float32)
    if cuts:
        values = values * steps_of(key, extent, cuts, -0.22, 0.18)
    return jnp.clip(values, -most, most).astype(kind)


def setup_inputs(seed: int = 0, part: int = 0) -> dict:
    streams_of = jax.random.split(jax.random.key(seed), 13)
    part_splits = jax.random.split(jax.random.fold_in(streams_of[12], part), 13)
    query_rows = draw_query_rows(jax.random.fold_in(jax.random.fold_in(streams_of[12], part), 71), part)
    row_key_value = draw_row_key_value(jax.random.fold_in(jax.random.fold_in(streams_of[12], part), 71), part)
    key_value_cache = draw_key_value_cache(jax.random.fold_in(jax.random.fold_in(streams_of[12], part), 71), part)
    resid = draw_resid(jax.random.fold_in(jax.random.fold_in(streams_of[12], part), 71), part)
    norm_gain = jnp.clip(1.0 + 0.1 * jax.random.normal(streams_of[4], (D,), jnp.float32), 0.5, 1.5)
    lengths = draw_lengths(jax.random.fold_in(jax.random.fold_in(streams_of[12], part), 71), part)
    positions = draw_positions(jax.random.fold_in(jax.random.fold_in(streams_of[12], part), 71), part)
    expert_ids_keys = jax.random.split(jax.random.fold_in(part_splits[7], 1), MASKED_ROWS // HALF_DOC_ROWS)
    expert_ids_turns = jax.random.permutation(jax.random.fold_in(part_splits[7], 3), MASKED_ROWS // HALF_DOC_ROWS)
    expert_ids = jax.vmap(lambda own, number: assign_block(jax.random.fold_in(part_splits[7], 2), own, number, HALF_DOC_ROWS, EXPERTS, TOP, MOST, 2))(expert_ids_keys, expert_ids_turns).reshape((MASKED_ROWS, TOP))
    gate_scores = jnp.clip(jnp.exp(math.log(1.0) - 2.3025851 * jax.random.uniform(part_splits[8], (MASKED_ROWS, TOP), jnp.float32) ** steps_of(part_splits[8], (MASKED_ROWS, TOP), ((0, 16),), -0.2, 0.2)), 0.1, 1.0)
    w_gate = gaussian(streams_of[9], (EXPERTS, D, FF), D ** -0.5, 0.125, ((0, 16),))
    w_up = gaussian(streams_of[10], (EXPERTS, D, FF), D ** -0.5, 0.125, ((0, 16),))
    w_down = gaussian(streams_of[11], (EXPERTS, FF, D), FF ** -0.5, 0.21875, ((0, 16),))
    return {"query_rows": query_rows, "row_key_value": row_key_value, "key_value_cache": key_value_cache, "resid": resid, "norm_gain": norm_gain, "lengths": lengths, "positions": positions, "expert_ids": expert_ids, "gate_scores": gate_scores, "w_gate": w_gate, "w_up": w_up, "w_down": w_down}


def single_document(element):
    query_tile_block, cache_rows, row_keys, length, marked = element
    key_value_width = KEY_VALUE_HEADS * HEAD_SIZE
    query_group_width = QUERY_HEADS // KEY_VALUE_HEADS
    document_rows = 2 * HALF_DOC_ROWS
    location = jnp.arange(2 * CACHED_POSITIONS, dtype=jnp.int32)
    is_marked = jnp.any(location[:, None] == marked[None, :].astype(jnp.int32), axis=1)
    usable = jnp.concatenate([(location < length.astype(jnp.int32)) & ~is_marked, jnp.ones((document_rows,), dtype=bool)])
    joined_parts = jnp.concatenate([cache_rows, row_keys], axis=0).astype(jnp.float32)
    key_portion = joined_parts[:, :key_value_width].reshape(-1, KEY_VALUE_HEADS, HEAD_SIZE)
    value_portion = joined_parts[:, key_value_width:].reshape(-1, KEY_VALUE_HEADS, HEAD_SIZE)
    query_head_rows = query_tile_block.astype(jnp.float32).reshape(document_rows, KEY_VALUE_HEADS, query_group_width, HEAD_SIZE)
    scores = jnp.einsum('mgqd,lgd->mgql', query_head_rows, key_portion, precision=lax.Precision.HIGHEST) * (1.0 / math.sqrt(HEAD_SIZE))
    scores = jnp.where(usable, scores, -1e+30)
    row_max = lax.optimization_barrier(jnp.max(scores, axis=-1, keepdims=True))
    weights = jnp.where(usable, jnp.exp(scores - row_max), 0.0)
    denominator = lax.optimization_barrier(jnp.sum(weights, axis=-1))
    rounded = lax.optimization_barrier(weights.astype(jnp.bfloat16)).astype(jnp.float32)
    summed = jnp.einsum('mgql,lgd->mgqd', rounded, value_portion, precision=lax.Precision.HIGHEST)
    attention_output = summed / denominator[..., None]
    return attention_output.reshape(document_rows, QUERY_HEADS * HEAD_SIZE).astype(jnp.bfloat16)

def reference(query_rows, row_key_value, key_value_cache, resid, norm_gain, lengths, positions, expert_ids, gate_scores, w_gate, w_up, w_down):
    document_rows = 2 * HALF_DOC_ROWS
    attention_output = lax.map(single_document, (query_rows.reshape(DOCUMENT_COUNT, document_rows, QUERY_HEADS * HEAD_SIZE), key_value_cache.reshape(DOCUMENT_COUNT, 2 * CACHED_POSITIONS, 2 * KEY_VALUE_HEADS * HEAD_SIZE), row_key_value.reshape(DOCUMENT_COUNT, document_rows, 2 * KEY_VALUE_HEADS * HEAD_SIZE), lengths, positions))
    attention_output = attention_output.reshape(MASKED_ROWS, QUERY_HEADS * HEAD_SIZE)
    residual = resid.astype(jnp.float32) + attention_output.astype(jnp.float32)
    normed = (residual * lax.rsqrt(lax.optimization_barrier(jnp.mean(residual * residual, axis=-1, keepdims=True)) + 1e-06) * norm_gain).astype(jnp.bfloat16)
    mix = gate_scores / lax.optimization_barrier(jnp.sum(gate_scores, axis=-1, keepdims=True))
    capacity = N_WIDE * MOST

    def one_expert(accumulator, expert_index):
        chosen = expert_ids == expert_index
        member = jnp.any(chosen, axis=-1)
        expert_share = lax.optimization_barrier(jnp.sum(jnp.where(chosen, mix, 0.0), axis=-1))
        gathered_order = jnp.argsort((~member).astype(jnp.int32), stable=True)[:capacity]
        picked = normed[gathered_order]
        gate_matrix = lax.dynamic_index_in_dim(w_gate, expert_index, 0, keepdims=False)
        up_matrix = lax.dynamic_index_in_dim(w_up, expert_index, 0, keepdims=False)
        down_matrix = lax.dynamic_index_in_dim(w_down, expert_index, 0, keepdims=False)
        gate_act = jnp.dot(picked, gate_matrix, preferred_element_type=jnp.float32)
        up_act = jnp.dot(picked, up_matrix, preferred_element_type=jnp.float32)
        hidden = (jax.nn.silu(gate_act) * up_act).astype(jnp.bfloat16)
        expert_out = jnp.dot(hidden, down_matrix, preferred_element_type=jnp.float32).astype(jnp.bfloat16)
        accumulator = accumulator.at[gathered_order].add(expert_share[gathered_order][:, None] * expert_out.astype(jnp.float32))
        return (accumulator, None)
    accumulator, unused = lax.scan(one_expert, jnp.zeros((MASKED_ROWS, D), jnp.float32), jnp.arange(EXPERTS, dtype=jnp.int32))
    return (residual + accumulator).astype(jnp.bfloat16)
```

```python
import functools
import math

import jax
import jax.numpy as jnp
from jax import lax
from jax.experimental import pallas as pl
from jax.experimental.pallas import tpu as pltpu
from jax.sharding import PartitionSpec as P

KEY_VALUE_HEADS = 4
HEAD_SIZE = 64
LANES = 128
NEVER = -1e30


def swapped(shard, axis, bit):
    return lax.ppermute(shard, axis, [(i, i ^ 1 << bit) for i in range(lax.axis_size(axis))])


def lane_index(shape):
    return lax.broadcasted_iota(jnp.int32, shape, 1)


def half_with_one(slab, odd):
    values = slab.astype(jnp.float32)
    if odd:
        values = pltpu.roll(values, HEAD_SIZE, 1)
    lane = lane_index(values.shape)
    return jnp.where(
        lane < HEAD_SIZE, values, jnp.where(lane == HEAD_SIZE, 1.0, 0.0)
    ).astype(jnp.bfloat16)


def attention_kernel(
    start_ref, length_ref, q_ref, cache_ref, rows_ref, marked_ref, out_ref, lse_ref,
    q_scr, k_scr, v_scr, s_scr,
):
    rows = q_ref.shape[0]
    span = cache_ref.shape[0]
    own = rows_ref.shape[0]
    keys = k_scr.shape[2]
    query_heads = q_ref.shape[1] // HEAD_SIZE
    width = KEY_VALUE_HEADS * HEAD_SIZE
    group = query_heads // KEY_VALUE_HEADS

    location = lane_index((1, keys))
    place = start_ref[0] + location
    hit = jnp.max(
        jnp.where(marked_ref[...] == place, 1.0, 0.0), axis=0, keepdims=True
    )
    in_cache = (place < length_ref[0]) & (hit == 0.0) & (location < span)
    usable = in_cache | ((location >= span) & (location < span + own))
    bias = jnp.where(usable, 0.0, NEVER)
    row = lax.broadcasted_iota(jnp.int32, (HEAD_SIZE, keys), 0)
    bias_rows = jnp.where(row == 0, bias, 0.0).astype(jnp.bfloat16)
    pad = keys - span - own
    for slab in range(KEY_VALUE_HEADS // 2):
        columns = slice(slab * LANES, (slab + 1) * LANES)
        value_columns = slice(width + slab * LANES, width + (slab + 1) * LANES)
        tail = [rows_ref[:, columns]]
        value_tail = [rows_ref[:, value_columns]]
        if pad:
            tail.append(jnp.zeros((pad, LANES), jnp.bfloat16))
            value_tail.append(jnp.zeros((pad, LANES), jnp.bfloat16))
        slab_keys = jnp.concatenate([cache_ref[:, columns]] + tail, axis=0).T
        slab_values = jnp.concatenate([cache_ref[:, value_columns]] + value_tail, axis=0)
        for odd in range(2):
            head = 2 * slab + odd
            k_scr[head, :HEAD_SIZE, :] = slab_keys[odd * HEAD_SIZE : (odd + 1) * HEAD_SIZE, :]
            k_scr[head, HEAD_SIZE:, :] = bias_rows
            v_scr[head] = half_with_one(slab_values, odd)
    for pair in range(query_heads // 2):
        slab = q_ref[:, pair * LANES : (pair + 1) * LANES].astype(jnp.float32) * (
            1.0 / math.sqrt(HEAD_SIZE)
        )
        for odd in range(2):
            q_scr[pair, odd * rows : (odd + 1) * rows, :] = half_with_one(slab, odd)

    pairs = query_heads // 2

    def scores(pair, slot):
        head = lax.div(pair, group // 2)
        s_scr[slot] = jnp.dot(q_scr[pair], k_scr[head], preferred_element_type=jnp.float32)

    def finish(pair, slot):
        head = lax.div(pair, group // 2)
        s = s_scr[slot]
        largest = jnp.max(s, axis=1, keepdims=True)
        p = jnp.exp(s - largest).astype(jnp.bfloat16)
        summed = jnp.dot(p, v_scr[head], preferred_element_type=jnp.float32)
        total = summed[:, HEAD_SIZE : HEAD_SIZE + 1]
        mean = summed / total
        lse = jnp.broadcast_to(largest + jnp.log(total), mean.shape)
        low = lane_index((rows, LANES)) < HEAD_SIZE
        out_ref[pair] = jnp.where(
            low, mean[:rows], pltpu.roll(mean[rows:], HEAD_SIZE, 1)
        ).astype(jnp.bfloat16)
        lse_ref[pair] = jnp.where(low, lse[:rows], lse[rows:])

    scores(0, 0)

    def step(j, unused):
        scores(2 * j + 1, 1)
        finish(2 * j, 0)
        scores(jnp.minimum(2 * j + 2, pairs - 1), 0)
        finish(2 * j + 1, 1)
        return unused

    lax.fori_loop(0, pairs // 2, step, 0)


def attention(queries, cache, row_key_value, start, length, marked):
    rows, width = queries.shape
    pairs = width // LANES
    keys = -(-(cache.shape[0] + row_key_value.shape[0]) // LANES) * LANES
    vmem = pl.BlockSpec(memory_space=pltpu.VMEM)
    smem = pl.BlockSpec(memory_space=pltpu.SMEM)
    return pl.pallas_call(
        attention_kernel,
        out_shape=(
            jax.ShapeDtypeStruct((pairs, rows, LANES), jnp.bfloat16),
            jax.ShapeDtypeStruct((pairs, rows, LANES), jnp.float32),
        ),
        in_specs=[smem, smem, vmem, vmem, vmem, vmem],
        out_specs=(vmem, vmem),
        scratch_shapes=[
            pltpu.VMEM((pairs, 2 * rows, LANES), jnp.bfloat16),
            pltpu.VMEM((KEY_VALUE_HEADS, LANES, keys), jnp.bfloat16),
            pltpu.VMEM((KEY_VALUE_HEADS, keys, LANES), jnp.bfloat16),
            pltpu.VMEM((2, 2 * rows, keys), jnp.float32),
        ],
        compiler_params=pltpu.CompilerParams(vmem_limit_bytes=40 * 1024 * 1024),
        cost_estimate=pl.CostEstimate(
            flops=4 * rows * width * keys,
            bytes_accessed=2 * cache.size + 8 * rows * width,
            transcendentals=rows * keys * width // HEAD_SIZE,
        ),
        name="attention",
    )(start, length, queries, cache, row_key_value, marked)


def local(
    query_rows,
    row_key_value,
    key_value_cache,
    resid,
    norm_gain,
    lengths,
    positions,
    expert_ids,
    gate_scores,
    w_gate,
    w_up,
    w_down,
):
    rows = query_rows.shape[0]
    width = query_rows.shape[1]
    span = key_value_cache.shape[0]
    device = lax.axis_index("wide")
    experts = lax.axis_size("wide")
    doc_index = device // 2
    half_index = device % 2

    mix = gate_scores / jnp.sum(gate_scores, axis=-1, keepdims=True)
    chosen = expert_ids[..., None] == jnp.arange(experts, dtype=jnp.int32)
    share = jnp.sum(jnp.where(chosen, mix[..., None], 0.0), axis=1)
    all_share = lax.all_gather(share, "wide", axis=0, tiled=True)

    length = lax.dynamic_slice_in_dim(lengths, doc_index, 1, 0)
    marked = lax.dynamic_index_in_dim(positions, doc_index, 0, keepdims=False)[:, None]
    visitor = swapped(query_rows, "wide", 0)
    start = jnp.reshape(half_index * span, (1,)).astype(jnp.int32)
    means, lse = attention(
        jnp.concatenate([query_rows, visitor], axis=0),
        key_value_cache, row_key_value, start, length, marked,
    )
    far_mean = swapped(means[:, rows:], "wide", 0).astype(jnp.float32)
    far_lse = swapped(lse[:, rows:], "wide", 0)
    own_mean = means[:, :rows].astype(jnp.float32)
    own_lse = lse[:, :rows]
    far_part = 1.0 / (1.0 + jnp.exp(own_lse - far_lse))
    merged = own_mean + (far_mean - own_mean) * far_part
    attended = jnp.swapaxes(merged, 0, 1).reshape(rows, width).astype(jnp.bfloat16)

    residual = resid.astype(jnp.float32) + attended.astype(jnp.float32)
    normed = (
        residual
        * lax.rsqrt(jnp.mean(residual * residual, axis=-1, keepdims=True) + 1e-06)
        * norm_gain
    ).astype(jnp.bfloat16)

    everyone = lax.all_gather(normed, "wide", axis=0, tiled=True)
    weight = lax.dynamic_slice_in_dim(all_share, device, 1, 1)
    gate_act = jnp.dot(everyone, w_gate[0], preferred_element_type=jnp.float32)
    up_act = jnp.dot(everyone, w_up[0], preferred_element_type=jnp.float32)
    hidden = (jax.nn.silu(gate_act) * up_act).astype(jnp.bfloat16)
    expert_out = jnp.dot(hidden, w_down[0], preferred_element_type=jnp.float32)
    weighted = (expert_out * weight).astype(jnp.bfloat16)
    routed = lax.psum_scatter(weighted, "wide", scatter_dimension=0, tiled=True)
    return (residual + routed.astype(jnp.float32)).astype(jnp.bfloat16)


def solution(mesh):
    return jax.shard_map(
        local,
        mesh=mesh,
        in_specs=(
            P(("grp", "wide"), None),
            P(("grp", "wide"), None),
            P(("grp", "wide"), None),
            P(("grp", "wide"), None),
            P(),
            P("grp"),
            P("grp", None),
            P(("grp", "wide"), None),
            P(("grp", "wide"), None),
            P("wide", None, None),
            P("wide", None, None),
            P("wide", None, None),
        ),
        out_specs=P(("grp", "wide"), None),
        check_vma=False,
    )
```

```python
import functools
import math

import jax
import jax.numpy as jnp
from jax import lax
from jax.experimental import pallas as pl
from jax.experimental.pallas import tpu as pltpu
from jax.sharding import PartitionSpec as P

KEY_VALUE_HEADS = 4
HEAD_SIZE = 64
LANES = 128
NEVER = -1e30


def swapped(shard, axis, bit):
    return lax.ppermute(shard, axis, [(i, i ^ 1 << bit) for i in range(lax.axis_size(axis))])


def lane_index(shape):
    return lax.broadcasted_iota(jnp.int32, shape, 1)


def half_with_one(slab, odd):
    values = slab.astype(jnp.float32)
    if odd:
        values = pltpu.roll(values, HEAD_SIZE, 1)
    lane = lane_index(values.shape)
    return jnp.where(
        lane < HEAD_SIZE, values, jnp.where(lane == HEAD_SIZE, 1.0, 0.0)
    ).astype(jnp.bfloat16)


def attention_kernel(
    start_ref, length_ref, q_ref, cache_ref, rows_ref, marked_ref, out_ref, lse_ref,
    q_scr, k_scr, v_scr, s_scr,
):
    rows = q_ref.shape[0]
    span = cache_ref.shape[0]
    own = rows_ref.shape[0]
    keys = k_scr.shape[2]
    query_heads = q_ref.shape[1] // HEAD_SIZE
    width = KEY_VALUE_HEADS * HEAD_SIZE
    group = query_heads // KEY_VALUE_HEADS

    location = lane_index((1, keys))
    place = start_ref[0] + location
    hit = jnp.max(
        jnp.where(marked_ref[...] == place, 1.0, 0.0), axis=0, keepdims=True
    )
    in_cache = (place < length_ref[0]) & (hit == 0.0) & (location < span)
    usable = in_cache | ((location >= span) & (location < span + own))
    bias = jnp.where(usable, 0.0, NEVER)
    row = lax.broadcasted_iota(jnp.int32, (HEAD_SIZE, keys), 0)
    bias_rows = jnp.where(row == 0, bias, 0.0).astype(jnp.bfloat16)
    pad = keys - span - own
    for slab in range(KEY_VALUE_HEADS // 2):
        columns = slice(slab * LANES, (slab + 1) * LANES)
        value_columns = slice(width + slab * LANES, width + (slab + 1) * LANES)
        tail = [rows_ref[:, columns]]
        value_tail = [rows_ref[:, value_columns]]
        if pad:
            tail.append(jnp.zeros((pad, LANES), jnp.bfloat16))
            value_tail.append(jnp.zeros((pad, LANES), jnp.bfloat16))
        slab_keys = jnp.concatenate([cache_ref[:, columns]] + tail, axis=0).T
        slab_values = jnp.concatenate([cache_ref[:, value_columns]] + value_tail, axis=0)
        for odd in range(2):
            head = 2 * slab + odd
            k_scr[head, :HEAD_SIZE, :] = slab_keys[odd * HEAD_SIZE : (odd + 1) * HEAD_SIZE, :]
            k_scr[head, HEAD_SIZE:, :] = bias_rows
            v_scr[head] = half_with_one(slab_values, odd)
    for pair in range(query_heads // 2):
        slab = q_ref[:, pair * LANES : (pair + 1) * LANES].astype(jnp.float32) * (
            1.0 / math.sqrt(HEAD_SIZE)
        )
        for odd in range(2):
            q_scr[pair, odd * rows : (odd + 1) * rows, :] = half_with_one(slab, odd)

    pairs = query_heads // 2

    def scores(pair, slot):
        head = lax.div(pair, group // 2)
        s_scr[slot] = jnp.dot(q_scr[pair], k_scr[head], preferred_element_type=jnp.float32)

    def finish(pair, slot):
        head = lax.div(pair, group // 2)
        s = s_scr[slot]
        largest = jnp.max(s, axis=1, keepdims=True)
        p = jnp.exp(s - largest).astype(jnp.bfloat16)
        summed = jnp.dot(p, v_scr[head], preferred_element_type=jnp.float32)
        total = summed[:, HEAD_SIZE : HEAD_SIZE + 1]
        mean = summed / total
        lse = jnp.broadcast_to(largest + jnp.log(total), mean.shape)
        low = lane_index((rows, LANES)) < HEAD_SIZE
        out_ref[pair] = jnp.where(
            low, mean[:rows], pltpu.roll(mean[rows:], HEAD_SIZE, 1)
        ).astype(jnp.bfloat16)
        lse_ref[pair] = jnp.where(low, lse[:rows], lse[rows:])

    scores(0, 0)

    def step(j, unused):
        scores(2 * j + 1, 1)
        finish(2 * j, 0)
        scores(jnp.minimum(2 * j + 2, pairs - 1), 0)
        finish(2 * j + 1, 1)
        return unused

    lax.fori_loop(0, pairs // 2, step, 0)


def attention(queries, cache, row_key_value, start, length, marked):
    rows, width = queries.shape
    pairs = width // LANES
    keys = -(-(cache.shape[0] + row_key_value.shape[0]) // LANES) * LANES
    vmem = pl.BlockSpec(memory_space=pltpu.VMEM)
    smem = pl.BlockSpec(memory_space=pltpu.SMEM)
    return pl.pallas_call(
        attention_kernel,
        out_shape=(
            jax.ShapeDtypeStruct((pairs, rows, LANES), jnp.bfloat16),
            jax.ShapeDtypeStruct((pairs, rows, LANES), jnp.float32),
        ),
        in_specs=[smem, smem, vmem, vmem, vmem, vmem],
        out_specs=(vmem, vmem),
        scratch_shapes=[
            pltpu.VMEM((pairs, 2 * rows, LANES), jnp.bfloat16),
            pltpu.VMEM((KEY_VALUE_HEADS, LANES, keys), jnp.bfloat16),
            pltpu.VMEM((KEY_VALUE_HEADS, keys, LANES), jnp.bfloat16),
            pltpu.VMEM((2, 2 * rows, keys), jnp.float32),
        ],
        compiler_params=pltpu.CompilerParams(vmem_limit_bytes=40 * 1024 * 1024),
        cost_estimate=pl.CostEstimate(
            flops=4 * rows * width * keys,
            bytes_accessed=2 * cache.size + 8 * rows * width,
            transcendentals=rows * keys * width // HEAD_SIZE,
        ),
        name="attention",
    )(start, length, queries, cache, row_key_value, marked)


def chip_at(place, chips):
    return jnp.where(place < chips // 2, 2 * place, 2 * (chips - 1 - place) + 1)


def place_of(chip, chips):
    return jnp.where(chip % 2 == 0, chip // 2, chips - 1 - chip // 2)


def experts_kernel(
    devices, first_ref, gate_hbm, up_hbm, down_hbm, out_ref,
    x, o, sibling_sums, ring_sums, hidden, w_gate, w_up, w_down,
    weight_sem, gather_send, gather_recv, share_send, share_recv,
    pair_send, pair_recv, ring_send, ring_recv,
):
    rows, half = first_ref.shape[0], first_ref.shape[0] // 2
    model = out_ref.shape[1]
    ff = w_down.shape[0]
    chips = devices // 2
    hops = chips // 2
    me = lax.axis_index("wide")
    core = me % 2
    place = place_of(me // 2, chips)
    sibling = me + 1 - 2 * core
    right = 2 * chip_at((place + 1) % chips, chips) + core
    left = 2 * chip_at((place + chips - 1) % chips, chips) + core

    def remote(source, target, send, recv, device):
        return pltpu.make_async_remote_copy(
            src_ref=source, dst_ref=target, send_sem=send, recv_sem=recv,
            device_id={"wide": device}, device_id_type=pl.DeviceIdType.MESH,
        )

    loads = [
        pltpu.make_async_copy(source.at[0], target, weight_sem.at[i])
        for i, (source, target) in enumerate(
            ((gate_hbm, w_gate), (up_hbm, w_up), (down_hbm, w_down))
        )
    ]
    for load in loads:
        load.start()
    x[0, :rows] = first_ref[...]
    ring_sums[hops - 1, half : rows + half] = jnp.zeros((rows, model), jnp.bfloat16)

    barrier = pltpu.get_barrier_semaphore()
    for neighbour in (left, right, sibling):
        pl.semaphore_signal(
            barrier, inc=1, device_id={"wide": neighbour}, device_id_type=pl.DeviceIdType.MESH
        )
    pl.semaphore_wait(barrier, 3)

    def gather(hop):
        if isinstance(hop, int) and hop == hops:
            top, bottom = pl.ds(0, half), pl.ds(half, half)
            from_left, from_right = top, bottom if hop == 1 else pl.ds(rows + half, half)
        else:
            top = bottom = None
            from_left, from_right = pl.ds(0, rows), pl.ds(rows, rows)
            if isinstance(hop, int) and hop == 1:
                from_right = pl.ds(0, rows)
        to_left = pl.ds(0, rows) if top is None else top
        to_right = pl.ds(rows, rows) if bottom is None else bottom
        return (
            remote(x.at[hop - 1, from_left], x.at[hop, to_left],
                   gather_send.at[0, hop], gather_recv.at[0, hop], right),
            remote(x.at[hop - 1, from_right], x.at[hop, to_right],
                   gather_send.at[1, hop], gather_recv.at[1, hop], left),
        )

    def share(hop, count):
        return remote(x.at[hop, pl.ds(0, count)], x.at[hop, pl.ds(count, count)],
                      share_send.at[hop], share_recv.at[hop], sibling)

    def pair(hop, count):
        return remote(o.at[hop, pl.ds(count, count)], sibling_sums.at[hop, pl.ds(0, count)],
                      pair_send.at[hop], pair_recv.at[hop], sibling)

    def ring(hop):
        if isinstance(hop, int) and hop == hops:
            go_left = land_left = pl.ds(0, half)
            go_right, land_right = pl.ds(half, half), pl.ds(rows + half, half)
        else:
            go_left = land_left = pl.ds(0, rows)
            go_right = land_right = pl.ds(rows, rows)
        return (
            remote(o.at[hop, go_left], ring_sums.at[hop - 1, land_left],
                   ring_send.at[0, hop], ring_recv.at[0, hop], left),
            remote(o.at[hop, go_right], ring_sums.at[hop - 1, land_right],
                   ring_send.at[1, hop], ring_recv.at[1, hop], right),
        )

    def chunk_of(size):
        return next(c for c in (256, 128, size) if size % c == 0)

    def run_experts(hop, count):
        tail = x[hop, :count, model:].astype(jnp.float32)
        lane = lane_index(tail.shape)
        weight = jnp.sum(
            jnp.where((lane == me) | (lane == devices + me), tail, 0.0), axis=1, keepdims=True
        )
        step = chunk_of(ff)

        def hide(i, unused):
            columns = pl.ds(pl.multiple_of(i * step, step), step)
            rows_in = x[hop, :count, :model]
            g = jnp.dot(rows_in, w_gate[:, columns], preferred_element_type=jnp.float32)
            u = jnp.dot(rows_in, w_up[:, columns], preferred_element_type=jnp.float32)
            hidden[:count, columns] = (g / (1.0 + jnp.exp(-g)) * u).astype(jnp.bfloat16)
            return unused

        lax.fori_loop(0, ff // step, hide, 0)
        wide = chunk_of(model)

        def expand(i, unused):
            columns = pl.ds(pl.multiple_of(i * wide, wide), wide)
            y = jnp.dot(hidden[:count], w_down[:, columns], preferred_element_type=jnp.float32)
            o[hop, :count, columns] = (y * weight).astype(jnp.bfloat16)
            return unused

        lax.fori_loop(0, model // wide, expand, 0)

    def start(copies):
        for copy in copies:
            copy.start()

    def arrive(hop, count, onward):
        for copy in gather(hop):
            copy.wait_recv()
        if onward is not None:
            start(gather(onward))
        share(hop, count).start()
        share(hop, count).wait_recv()
        run_experts(hop, 2 * count)
        pair(hop, count).start()

    start(gather(1))
    share(0, rows).start()
    for load in loads:
        load.wait()
    share(0, rows).wait_recv()
    run_experts(0, 2 * rows)
    pair(0, rows).start()

    def middle(hop, unused):
        arrive(hop, 2 * rows, hop + 1)
        return unused

    lax.fori_loop(1, hops - 1, middle, 0)
    if hops > 1:
        arrive(hops - 1, 2 * rows, hops)
    arrive(hops, rows, None)

    pair(hops, rows).wait_recv()
    o[hops, :rows] = (
        o[hops, :rows].astype(jnp.float32) + sibling_sums[hops, :rows].astype(jnp.float32)
    ).astype(jnp.bfloat16)
    start(ring(hops))

    def add_up(hop):
        pair(hop, 2 * rows).wait_recv()
        for copy in ring(hops if isinstance(hop, int) and hop == hops - 1 else hop + 1):
            copy.wait_recv()
        o[hop, : 2 * rows] = (
            o[hop, : 2 * rows].astype(jnp.float32)
            + sibling_sums[hop].astype(jnp.float32)
            + ring_sums[hop].astype(jnp.float32)
        ).astype(jnp.bfloat16)
        start(ring(hop))

    if hops > 1:
        add_up(hops - 1)

    def nearer(i, unused):
        add_up(hops - 2 - i)
        return unused

    lax.fori_loop(0, hops - 2, nearer, 0)
    pair(0, rows).wait_recv()
    for copy in ring(1):
        copy.wait_recv()
    out_ref[...] = (
        o[0, :rows].astype(jnp.float32)
        + sibling_sums[0, :rows].astype(jnp.float32)
        + ring_sums[0, :rows].astype(jnp.float32)
        + ring_sums[0, rows:].astype(jnp.float32)
    )

    def sent(hop, count):
        for copy in gather(hop) + ring(hop) + (share(hop, count), pair(hop, count)):
            copy.wait_send()

    share(0, rows).wait_send()
    pair(0, rows).wait_send()
    if hops > 1:
        sent(1, 2 * rows)

    def drain(hop, unused):
        sent(hop, 2 * rows)
        return unused

    lax.fori_loop(2, hops, drain, 0)
    sent(hops, rows)


def scratch_of(rows, wide, model, ff, devices):
    hops = devices // 4
    return [
        ((hops + 1, 4 * rows, wide), jnp.bfloat16),
        ((hops + 1, 4 * rows, model), jnp.bfloat16),
        ((hops + 1, 2 * rows, model), jnp.bfloat16),
        ((hops, 2 * rows, model), jnp.bfloat16),
        ((4 * rows, ff), jnp.bfloat16),
        ((model, ff), jnp.bfloat16),
        ((model, ff), jnp.bfloat16),
        ((ff, model), jnp.bfloat16),
    ]


def fits(buffers):
    return sum(2 * math.prod(shape) for shape, unused in buffers) < 44 * 1024 * 1024


def routed_experts(first, w_gate, w_up, w_down, devices):
    rows, wide = first.shape
    model, ff = w_gate.shape[1:]
    hops = devices // 4
    anywhere = pl.BlockSpec(memory_space=pl.ANY)
    vmem = pl.BlockSpec(memory_space=pltpu.VMEM)
    dma = pltpu.SemaphoreType.DMA
    return pl.pallas_call(
        functools.partial(experts_kernel, devices),
        out_shape=jax.ShapeDtypeStruct((rows, model), jnp.float32),
        in_specs=[vmem, anywhere, anywhere, anywhere],
        out_specs=vmem,
        scratch_shapes=[
            pltpu.VMEM(shape, kind)
            for shape, kind in scratch_of(rows, wide, model, ff, devices)
        ]
        + [dma((3,))]
        + [dma((2, hops + 1)), dma((2, hops + 1)), dma((hops + 1,)), dma((hops + 1,))]
        + [dma((hops + 1,)), dma((hops + 1,)), dma((2, hops + 1)), dma((2, hops + 1))],
        compiler_params=pltpu.CompilerParams(
            collective_id=0, has_side_effects=True, vmem_limit_bytes=56 * 1024 * 1024
        ),
        cost_estimate=pl.CostEstimate(
            flops=6 * rows * devices * model * ff,
            bytes_accessed=6 * model * ff,
            transcendentals=rows * devices * ff,
        ),
        name="experts",
    )(first, w_gate, w_up, w_down)


def local(
    query_rows,
    row_key_value,
    key_value_cache,
    resid,
    norm_gain,
    lengths,
    positions,
    expert_ids,
    gate_scores,
    w_gate,
    w_up,
    w_down,
):
    rows = query_rows.shape[0]
    width = query_rows.shape[1]
    span = key_value_cache.shape[0]
    device = lax.axis_index("wide")
    experts = lax.axis_size("wide")
    doc_index = device // 2
    half_index = device % 2

    mix = gate_scores / jnp.sum(gate_scores, axis=-1, keepdims=True)
    chosen = expert_ids[..., None] == jnp.arange(experts, dtype=jnp.int32)
    share = jnp.sum(jnp.where(chosen, mix[..., None], 0.0), axis=1)
    high = share.astype(jnp.bfloat16)
    low = (share - high.astype(jnp.float32)).astype(jnp.bfloat16)
    spare = -(2 * experts) % LANES
    shares = jnp.concatenate([high, low, jnp.zeros((rows, spare), jnp.bfloat16)], axis=1)

    length = lax.dynamic_slice_in_dim(lengths, doc_index, 1, 0)
    marked = lax.dynamic_index_in_dim(positions, doc_index, 0, keepdims=False)[:, None]
    visitor = swapped(query_rows, "wide", 0)
    start = jnp.reshape(half_index * span, (1,)).astype(jnp.int32)
    means, lse = attention(
        jnp.concatenate([query_rows, visitor], axis=0),
        key_value_cache, row_key_value, start, length, marked,
    )
    far_mean = swapped(means[:, rows:], "wide", 0).astype(jnp.float32)
    far_lse = swapped(lse[:, rows:], "wide", 0)
    own_mean = means[:, :rows].astype(jnp.float32)
    own_lse = lse[:, :rows]
    far_part = 1.0 / (1.0 + jnp.exp(own_lse - far_lse))
    merged = own_mean + (far_mean - own_mean) * far_part
    attended = jnp.swapaxes(merged, 0, 1).reshape(rows, width).astype(jnp.bfloat16)

    residual = resid.astype(jnp.float32) + attended.astype(jnp.float32)
    normed = (
        residual
        * lax.rsqrt(jnp.mean(residual * residual, axis=-1, keepdims=True) + 1e-06)
        * norm_gain
    ).astype(jnp.bfloat16)

    first = jnp.concatenate([normed, shares], axis=1)
    model, ff = w_gate.shape[1:]
    if experts % 4 == 0 and fits(scratch_of(rows, first.shape[1], model, ff, experts)):
        routed = routed_experts(first, w_gate, w_up, w_down, experts)
        return (residual + routed).astype(jnp.bfloat16)

    gathered = lax.all_gather(first, "wide", axis=0, tiled=True)
    everyone = gathered[:, :model]
    weight = sum(
        lax.dynamic_slice_in_dim(gathered, model + device + part * experts, 1, 1).astype(
            jnp.float32
        )
        for part in range(2)
    )
    gate_act = jnp.dot(everyone, w_gate[0], preferred_element_type=jnp.float32)
    up_act = jnp.dot(everyone, w_up[0], preferred_element_type=jnp.float32)
    hidden = (jax.nn.silu(gate_act) * up_act).astype(jnp.bfloat16)
    expert_out = jnp.dot(hidden, w_down[0], preferred_element_type=jnp.float32)
    weighted = (expert_out * weight).astype(jnp.bfloat16)
    routed = lax.psum_scatter(weighted, "wide", scatter_dimension=0, tiled=True)
    return (residual + routed.astype(jnp.float32)).astype(jnp.bfloat16)


def solution(mesh):
    return jax.shard_map(
        local,
        mesh=mesh,
        in_specs=(
            P(("grp", "wide"), None),
            P(("grp", "wide"), None),
            P(("grp", "wide"), None),
            P(("grp", "wide"), None),
            P(),
            P("grp"),
            P("grp", None),
            P(("grp", "wide"), None),
            P(("grp", "wide"), None),
            P("wide", None, None),
            P("wide", None, None),
            P("wide", None, None),
        ),
        out_specs=P(("grp", "wide"), None),
        check_vma=False,
    )
```

```python
import functools
import math

import jax
import jax.numpy as jnp
from jax import lax
from jax.experimental import pallas as pl
from jax.experimental.pallas import tpu as pltpu
from jax.sharding import PartitionSpec as P

KEY_VALUE_HEADS = 4
HEAD_SIZE = 64
LANES = 128
NEVER = -1e30


def swapped(shard, axis, bit):
    return lax.ppermute(shard, axis, [(i, i ^ 1 << bit) for i in range(lax.axis_size(axis))])


def lane_index(shape):
    return lax.broadcasted_iota(jnp.int32, shape, 1)


def half_with_one(slab, odd):
    values = slab.astype(jnp.float32)
    if odd:
        values = pltpu.roll(values, HEAD_SIZE, 1)
    lane = lane_index(values.shape)
    return jnp.where(
        lane < HEAD_SIZE, values, jnp.where(lane == HEAD_SIZE, 1.0, 0.0)
    ).astype(jnp.bfloat16)


def attention_kernel(
    start_ref, length_ref, q_ref, cache_ref, rows_ref, marked_ref, out_ref, lse_ref,
    q_scr, k_scr, v_scr, s_scr,
):
    rows = q_ref.shape[0]
    span = cache_ref.shape[0]
    own = rows_ref.shape[0]
    keys = k_scr.shape[2]
    query_heads = q_ref.shape[1] // HEAD_SIZE
    width = KEY_VALUE_HEADS * HEAD_SIZE
    group = query_heads // KEY_VALUE_HEADS

    location = lane_index((1, keys))
    place = start_ref[0] + location
    hit = jnp.max(
        jnp.where(marked_ref[...] == place, 1.0, 0.0), axis=0, keepdims=True
    )
    in_cache = (place < length_ref[0]) & (hit == 0.0) & (location < span)
    usable = in_cache | ((location >= span) & (location < span + own))
    bias = jnp.where(usable, 0.0, NEVER)
    row = lax.broadcasted_iota(jnp.int32, (HEAD_SIZE, keys), 0)
    bias_rows = jnp.where(row == 0, bias, 0.0).astype(jnp.bfloat16)
    pad = keys - span - own
    for slab in range(KEY_VALUE_HEADS // 2):
        columns = slice(slab * LANES, (slab + 1) * LANES)
        value_columns = slice(width + slab * LANES, width + (slab + 1) * LANES)
        tail = [rows_ref[:, columns]]
        value_tail = [rows_ref[:, value_columns]]
        if pad:
            tail.append(jnp.zeros((pad, LANES), jnp.bfloat16))
            value_tail.append(jnp.zeros((pad, LANES), jnp.bfloat16))
        slab_keys = jnp.concatenate([cache_ref[:, columns]] + tail, axis=0).T
        slab_values = jnp.concatenate([cache_ref[:, value_columns]] + value_tail, axis=0)
        for odd in range(2):
            head = 2 * slab + odd
            k_scr[head, :HEAD_SIZE, :] = slab_keys[odd * HEAD_SIZE : (odd + 1) * HEAD_SIZE, :]
            k_scr[head, HEAD_SIZE:, :] = bias_rows
            v_scr[head] = half_with_one(slab_values, odd)
    for pair in range(query_heads // 2):
        slab = q_ref[:, pair * LANES : (pair + 1) * LANES].astype(jnp.float32) * (
            1.0 / math.sqrt(HEAD_SIZE)
        )
        for odd in range(2):
            q_scr[pair, odd * rows : (odd + 1) * rows, :] = half_with_one(slab, odd)

    pairs = query_heads // 2

    def scores(pair, slot):
        head = lax.div(pair, group // 2)
        s_scr[slot] = jnp.dot(q_scr[pair], k_scr[head], preferred_element_type=jnp.float32)

    def finish(pair, slot):
        head = lax.div(pair, group // 2)
        s = s_scr[slot]
        largest = jnp.max(s, axis=1, keepdims=True)
        p = jnp.exp(s - largest).astype(jnp.bfloat16)
        summed = jnp.dot(p, v_scr[head], preferred_element_type=jnp.float32)
        total = summed[:, HEAD_SIZE : HEAD_SIZE + 1]
        mean = summed / total
        lse = jnp.broadcast_to(largest + jnp.log(total), mean.shape)
        low = lane_index((rows, LANES)) < HEAD_SIZE
        out_ref[pair] = jnp.where(
            low, mean[:rows], pltpu.roll(mean[rows:], HEAD_SIZE, 1)
        ).astype(jnp.bfloat16)
        lse_ref[pair] = jnp.where(low, lse[:rows], lse[rows:])

    scores(0, 0)

    def step(j, unused):
        scores(2 * j + 1, 1)
        finish(2 * j, 0)
        scores(jnp.minimum(2 * j + 2, pairs - 1), 0)
        finish(2 * j + 1, 1)
        return unused

    lax.fori_loop(0, pairs // 2, step, 0)


def attention(queries, cache, row_key_value, start, length, marked):
    rows, width = queries.shape
    pairs = width // LANES
    keys = -(-(cache.shape[0] + row_key_value.shape[0]) // LANES) * LANES
    vmem = pl.BlockSpec(memory_space=pltpu.VMEM)
    smem = pl.BlockSpec(memory_space=pltpu.SMEM)
    return pl.pallas_call(
        attention_kernel,
        out_shape=(
            jax.ShapeDtypeStruct((pairs, rows, LANES), jnp.bfloat16),
            jax.ShapeDtypeStruct((pairs, rows, LANES), jnp.float32),
        ),
        in_specs=[smem, smem, vmem, vmem, vmem, vmem],
        out_specs=(vmem, vmem),
        scratch_shapes=[
            pltpu.VMEM((pairs, 2 * rows, LANES), jnp.bfloat16),
            pltpu.VMEM((KEY_VALUE_HEADS, LANES, keys), jnp.bfloat16),
            pltpu.VMEM((KEY_VALUE_HEADS, keys, LANES), jnp.bfloat16),
            pltpu.VMEM((2, 2 * rows, keys), jnp.float32),
        ],
        compiler_params=pltpu.CompilerParams(vmem_limit_bytes=40 * 1024 * 1024),
        cost_estimate=pl.CostEstimate(
            flops=4 * rows * width * keys,
            bytes_accessed=2 * cache.size + 8 * rows * width,
            transcendentals=rows * keys * width // HEAD_SIZE,
        ),
        name="attention",
    )(start, length, queries, cache, row_key_value, marked)


def chip_at(place, chips):
    return jnp.where(place < chips // 2, 2 * place, 2 * (chips - 1 - place) + 1)


def place_of(chip, chips):
    return jnp.where(chip % 2 == 0, chip // 2, chips - 1 - chip // 2)


def experts_kernel(
    devices, first_ref, gate_hbm, up_hbm, down_hbm, out_ref,
    x, o, sibling_sums, ring_sums, hidden, w_gate, w_up, w_down,
    weight_sem, gather_send, gather_recv, share_send, share_recv,
    pair_send, pair_recv, ring_send, ring_recv,
):
    rows, half = first_ref.shape[0], first_ref.shape[0] // 2
    model = out_ref.shape[1]
    ff = w_down.shape[0]
    chips = devices // 2
    hops = chips // 2
    me = lax.axis_index("wide")
    core = me % 2
    place = place_of(me // 2, chips)
    sibling = me + 1 - 2 * core
    right = 2 * chip_at((place + 1) % chips, chips) + core
    left = 2 * chip_at((place + chips - 1) % chips, chips) + core

    def remote(source, target, send, recv, device):
        return pltpu.make_async_remote_copy(
            src_ref=source, dst_ref=target, send_sem=send, recv_sem=recv,
            device_id={"wide": device}, device_id_type=pl.DeviceIdType.MESH,
        )

    parts = (pl.ds(0, model // 2), pl.ds(model // 2, model // 2))
    wide_parts = (pl.ds(0, model // 2), pl.ds(model // 2, x.shape[2] - model // 2))

    loads = [
        pltpu.make_async_copy(source.at[0], target, weight_sem.at[i])
        for i, (source, target) in enumerate(
            ((gate_hbm, w_gate), (up_hbm, w_up), (down_hbm, w_down))
        )
    ]
    for load in loads:
        load.start()
    x[0, :rows] = first_ref[...]
    ring_sums[hops - 1, half : rows + half] = jnp.zeros((rows, model), jnp.bfloat16)

    barrier = pltpu.get_barrier_semaphore()
    for neighbour in (left, right, sibling):
        pl.semaphore_signal(
            barrier, inc=1, device_id={"wide": neighbour}, device_id_type=pl.DeviceIdType.MESH
        )
    pl.semaphore_wait(barrier, 3)

    def gather(hop, part):
        if isinstance(hop, int) and hop == hops:
            top, bottom = pl.ds(0, half), pl.ds(half, half)
            from_left, from_right = top, bottom if hop == 1 else pl.ds(rows + half, half)
        else:
            top = bottom = None
            from_left, from_right = pl.ds(0, rows), pl.ds(rows, rows)
            if isinstance(hop, int) and hop == 1:
                from_right = pl.ds(0, rows)
        to_left = pl.ds(0, rows) if top is None else top
        to_right = pl.ds(rows, rows) if bottom is None else bottom
        columns = wide_parts[part]
        return (
            remote(x.at[hop - 1, from_left, columns], x.at[hop, to_left, columns],
                   gather_send.at[0, part, hop], gather_recv.at[0, part, hop], right),
            remote(x.at[hop - 1, from_right, columns], x.at[hop, to_right, columns],
                   gather_send.at[1, part, hop], gather_recv.at[1, part, hop], left),
        )

    def share(hop, count, part):
        return remote(x.at[hop, pl.ds(0, count), wide_parts[part]],
                      x.at[hop, pl.ds(count, count), wide_parts[part]],
                      share_send.at[part, hop], share_recv.at[part, hop], sibling)

    def pair(hop, count, part):
        return remote(o.at[hop, pl.ds(count, count), parts[part]],
                      sibling_sums.at[hop, pl.ds(0, count), parts[part]],
                      pair_send.at[part, hop], pair_recv.at[part, hop], sibling)

    def ring(hop, part):
        if isinstance(hop, int) and hop == hops:
            go_left = land_left = pl.ds(0, half)
            go_right, land_right = pl.ds(half, half), pl.ds(rows + half, half)
        else:
            go_left = land_left = pl.ds(0, rows)
            go_right = land_right = pl.ds(rows, rows)
        columns = parts[part]
        return (
            remote(o.at[hop, go_left, columns], ring_sums.at[hop - 1, land_left, columns],
                   ring_send.at[0, part, hop], ring_recv.at[0, part, hop], left),
            remote(o.at[hop, go_right, columns], ring_sums.at[hop - 1, land_right, columns],
                   ring_send.at[1, part, hop], ring_recv.at[1, part, hop], right),
        )

    def chunk_of(size):
        return next(c for c in (256, 128, size) if size % c == 0)

    def run_experts(hop, count):
        tail = x[hop, :count, model:].astype(jnp.float32)
        lane = lane_index(tail.shape)
        weight = jnp.sum(
            jnp.where((lane == me) | (lane == devices + me), tail, 0.0), axis=1, keepdims=True
        )
        step = chunk_of(ff)

        def hide(i, unused):
            columns = pl.ds(pl.multiple_of(i * step, step), step)
            rows_in = x[hop, :count, :model]
            g = jnp.dot(rows_in, w_gate[:, columns], preferred_element_type=jnp.float32)
            u = jnp.dot(rows_in, w_up[:, columns], preferred_element_type=jnp.float32)
            hidden[:count, columns] = (g / (1.0 + jnp.exp(-g)) * u).astype(jnp.bfloat16)
            return unused

        lax.fori_loop(0, ff // step, hide, 0, unroll=True)
        wide = chunk_of(model // 2)

        for part in range(2):

            def expand(i, unused):
                first_column = part * (model // 2) + i * wide
                columns = pl.ds(pl.multiple_of(first_column, wide), wide)
                y = jnp.dot(
                    hidden[:count], w_down[:, columns], preferred_element_type=jnp.float32
                )
                o[hop, :count, columns] = (y * weight).astype(jnp.bfloat16)
                return unused

            lax.fori_loop(0, model // 2 // wide, expand, 0, unroll=True)
            pair(hop, count // 2, part).start()

    def arrive(hop, count, onward):
        for part in range(2):
            coming = gather(hop, part)
            going = (None, None) if onward is None else gather(onward, part)
            for come, go in zip(coming, going):
                come.wait_recv()
                if go is not None:
                    go.start()
            share(hop, count, part).start()
        for part in range(2):
            share(hop, count, part).wait_recv()
        run_experts(hop, 2 * count)

    for part in range(2):
        for copy in gather(1, part):
            copy.start()
    for part in range(2):
        share(0, rows, part).start()
    for load in loads:
        load.wait()
    for part in range(2):
        share(0, rows, part).wait_recv()
    run_experts(0, 2 * rows)

    def middle(hop, unused):
        arrive(hop, 2 * rows, hop + 1)
        return unused

    lax.fori_loop(1, hops - 1, middle, 0)
    if hops > 1:
        arrive(hops - 1, 2 * rows, hops)
    arrive(hops, rows, None)

    def wider(ref, hop, some, columns):
        return ref[hop, some, columns].astype(jnp.float32)

    for part, columns in enumerate(parts):
        pair(hops, rows, part).wait_recv()
        some = pl.ds(0, rows)
        o[hops, some, columns] = (
            wider(o, hops, some, columns) + wider(sibling_sums, hops, some, columns)
        ).astype(jnp.bfloat16)
        for copy in ring(hops, part):
            copy.start()

    def add_up(hop):
        further = hops if isinstance(hop, int) and hop == hops - 1 else hop + 1
        for part, columns in enumerate(parts):
            pair(hop, 2 * rows, part).wait_recv()
            for side, (come, go) in enumerate(zip(ring(further, part), ring(hop, part))):
                come.wait_recv()
                some = pl.ds(side * rows, rows)
                o[hop, some, columns] = (
                    wider(o, hop, some, columns)
                    + wider(sibling_sums, hop, some, columns)
                    + wider(ring_sums, hop, some, columns)
                ).astype(jnp.bfloat16)
                go.start()

    if hops > 1:
        add_up(hops - 1)

    def nearer(i, unused):
        add_up(hops - 2 - i)
        return unused

    lax.fori_loop(0, hops - 2, nearer, 0)
    for part, columns in enumerate(parts):
        pair(0, rows, part).wait_recv()
        for copy in ring(1, part):
            copy.wait_recv()
        some, rest = pl.ds(0, rows), pl.ds(rows, rows)
        out_ref[:, columns] = (
            wider(o, 0, some, columns)
            + wider(sibling_sums, 0, some, columns)
            + wider(ring_sums, 0, some, columns)
            + wider(ring_sums, 0, rest, columns)
        )

    def sent(hop, count):
        for part in range(2):
            for copy in gather(hop, part) + ring(hop, part):
                copy.wait_send()
            share(hop, count, part).wait_send()
            pair(hop, count, part).wait_send()

    for part in range(2):
        share(0, rows, part).wait_send()
        pair(0, rows, part).wait_send()
    if hops > 1:
        sent(1, 2 * rows)

    def drain(hop, unused):
        sent(hop, 2 * rows)
        return unused

    lax.fori_loop(2, hops, drain, 0)
    sent(hops, rows)


def scratch_of(rows, wide, model, ff, devices):
    hops = devices // 4
    return [
        ((hops + 1, 4 * rows, wide), jnp.bfloat16),
        ((hops + 1, 4 * rows, model), jnp.bfloat16),
        ((hops + 1, 2 * rows, model), jnp.bfloat16),
        ((hops, 2 * rows, model), jnp.bfloat16),
        ((4 * rows, ff), jnp.bfloat16),
        ((model, ff), jnp.bfloat16),
        ((model, ff), jnp.bfloat16),
        ((ff, model), jnp.bfloat16),
    ]


def fits(buffers):
    return sum(2 * math.prod(shape) for shape, unused in buffers) < 44 * 1024 * 1024


def routed_experts(first, w_gate, w_up, w_down, devices):
    rows, wide = first.shape
    model, ff = w_gate.shape[1:]
    hops = devices // 4
    anywhere = pl.BlockSpec(memory_space=pl.ANY)
    vmem = pl.BlockSpec(memory_space=pltpu.VMEM)
    dma = pltpu.SemaphoreType.DMA
    return pl.pallas_call(
        functools.partial(experts_kernel, devices),
        out_shape=jax.ShapeDtypeStruct((rows, model), jnp.float32),
        in_specs=[vmem, anywhere, anywhere, anywhere],
        out_specs=vmem,
        scratch_shapes=[
            pltpu.VMEM(shape, kind)
            for shape, kind in scratch_of(rows, wide, model, ff, devices)
        ]
        + [dma((3,))]
        + [dma((2, 2, hops + 1)), dma((2, 2, hops + 1)), dma((2, hops + 1)), dma((2, hops + 1))]
        + [dma((2, hops + 1)), dma((2, hops + 1)), dma((2, 2, hops + 1)), dma((2, 2, hops + 1))],
        compiler_params=pltpu.CompilerParams(
            collective_id=0, has_side_effects=True, vmem_limit_bytes=56 * 1024 * 1024
        ),
        cost_estimate=pl.CostEstimate(
            flops=6 * rows * devices * model * ff,
            bytes_accessed=6 * model * ff,
            transcendentals=rows * devices * ff,
        ),
        name="experts",
    )(first, w_gate, w_up, w_down)


def local(
    query_rows,
    row_key_value,
    key_value_cache,
    resid,
    norm_gain,
    lengths,
    positions,
    expert_ids,
    gate_scores,
    w_gate,
    w_up,
    w_down,
):
    rows = query_rows.shape[0]
    width = query_rows.shape[1]
    span = key_value_cache.shape[0]
    device = lax.axis_index("wide")
    experts = lax.axis_size("wide")
    doc_index = device // 2
    half_index = device % 2

    mix = gate_scores / jnp.sum(gate_scores, axis=-1, keepdims=True)
    chosen = expert_ids[..., None] == jnp.arange(experts, dtype=jnp.int32)
    share = jnp.sum(jnp.where(chosen, mix[..., None], 0.0), axis=1)
    high = share.astype(jnp.bfloat16)
    low = (share - high.astype(jnp.float32)).astype(jnp.bfloat16)
    spare = -(2 * experts) % LANES
    shares = jnp.concatenate([high, low, jnp.zeros((rows, spare), jnp.bfloat16)], axis=1)

    length = lax.dynamic_slice_in_dim(lengths, doc_index, 1, 0)
    marked = lax.dynamic_index_in_dim(positions, doc_index, 0, keepdims=False)[:, None]
    visitor = swapped(query_rows, "wide", 0)
    start = jnp.reshape(half_index * span, (1,)).astype(jnp.int32)
    means, lse = attention(
        jnp.concatenate([query_rows, visitor], axis=0),
        key_value_cache, row_key_value, start, length, marked,
    )
    far_mean = swapped(means[:, rows:], "wide", 0).astype(jnp.float32)
    far_lse = swapped(lse[:, rows:], "wide", 0)
    own_mean = means[:, :rows].astype(jnp.float32)
    own_lse = lse[:, :rows]
    far_part = 1.0 / (1.0 + jnp.exp(own_lse - far_lse))
    merged = own_mean + (far_mean - own_mean) * far_part
    attended = jnp.swapaxes(merged, 0, 1).reshape(rows, width).astype(jnp.bfloat16)

    residual = resid.astype(jnp.float32) + attended.astype(jnp.float32)
    normed = (
        residual
        * lax.rsqrt(jnp.mean(residual * residual, axis=-1, keepdims=True) + 1e-06)
        * norm_gain
    ).astype(jnp.bfloat16)

    first = jnp.concatenate([normed, shares], axis=1)
    model, ff = w_gate.shape[1:]
    if experts % 4 == 0 and fits(scratch_of(rows, first.shape[1], model, ff, experts)):
        routed = routed_experts(first, w_gate, w_up, w_down, experts)
        return (residual + routed).astype(jnp.bfloat16)

    gathered = lax.all_gather(first, "wide", axis=0, tiled=True)
    everyone = gathered[:, :model]
    weight = sum(
        lax.dynamic_slice_in_dim(gathered, model + device + part * experts, 1, 1).astype(
            jnp.float32
        )
        for part in range(2)
    )
    gate_act = jnp.dot(everyone, w_gate[0], preferred_element_type=jnp.float32)
    up_act = jnp.dot(everyone, w_up[0], preferred_element_type=jnp.float32)
    hidden = (jax.nn.silu(gate_act) * up_act).astype(jnp.bfloat16)
    expert_out = jnp.dot(hidden, w_down[0], preferred_element_type=jnp.float32)
    weighted = (expert_out * weight).astype(jnp.bfloat16)
    routed = lax.psum_scatter(weighted, "wide", scatter_dimension=0, tiled=True)
    return (residual + routed.astype(jnp.float32)).astype(jnp.bfloat16)


def solution(mesh):
    return jax.shard_map(
        local,
        mesh=mesh,
        in_specs=(
            P(("grp", "wide"), None),
            P(("grp", "wide"), None),
            P(("grp", "wide"), None),
            P(("grp", "wide"), None),
            P(),
            P("grp"),
            P("grp", None),
            P(("grp", "wide"), None),
            P(("grp", "wide"), None),
            P("wide", None, None),
            P("wide", None, None),
            P("wide", None, None),
        ),
        out_specs=P(("grp", "wide"), None),
        check_vma=False,
    )
```

```python
import functools
import math

import jax
import jax.numpy as jnp
from jax import lax
from jax.experimental import pallas as pl
from jax.experimental.pallas import tpu as pltpu
from jax.sharding import PartitionSpec as P

KEY_VALUE_HEADS = 4
HEAD_SIZE = 64
LANES = 128
NEVER = -1e30


def swapped(shard, axis, bit):
    return lax.ppermute(shard, axis, [(i, i ^ 1 << bit) for i in range(lax.axis_size(axis))])


def lane_index(shape):
    return lax.broadcasted_iota(jnp.int32, shape, 1)


def half_with_one(slab, odd):
    values = slab.astype(jnp.float32)
    if odd:
        values = pltpu.roll(values, HEAD_SIZE, 1)
    lane = lane_index(values.shape)
    return jnp.where(
        lane < HEAD_SIZE, values, jnp.where(lane == HEAD_SIZE, 1.0, 0.0)
    ).astype(jnp.bfloat16)


def place_keys(start_ref, length_ref, cache_ref, rows_ref, marked_ref, k_scr, v_scr):
    span = cache_ref.shape[0]
    own = rows_ref.shape[0]
    keys = k_scr.shape[2]
    width = KEY_VALUE_HEADS * HEAD_SIZE

    location = lane_index((1, keys))
    place = start_ref[0] + location
    hit = jnp.max(
        jnp.where(marked_ref[...] == place, 1.0, 0.0), axis=0, keepdims=True
    )
    in_cache = (place < length_ref[0]) & (hit == 0.0) & (location < span)
    usable = in_cache | ((location >= span) & (location < span + own))
    bias = jnp.where(usable, 0.0, NEVER)
    row = lax.broadcasted_iota(jnp.int32, (HEAD_SIZE, keys), 0)
    bias_rows = jnp.where(row == 0, bias, 0.0).astype(jnp.bfloat16)
    pad = keys - span - own
    for slab in range(KEY_VALUE_HEADS // 2):
        columns = slice(slab * LANES, (slab + 1) * LANES)
        value_columns = slice(width + slab * LANES, width + (slab + 1) * LANES)
        tail = [rows_ref[:, columns]]
        value_tail = [rows_ref[:, value_columns]]
        if pad:
            tail.append(jnp.zeros((pad, LANES), jnp.bfloat16))
            value_tail.append(jnp.zeros((pad, LANES), jnp.bfloat16))
        slab_keys = jnp.concatenate([cache_ref[:, columns]] + tail, axis=0).T
        slab_values = jnp.concatenate([cache_ref[:, value_columns]] + value_tail, axis=0)
        for odd in range(2):
            head = 2 * slab + odd
            k_scr[head, :HEAD_SIZE, :] = slab_keys[odd * HEAD_SIZE : (odd + 1) * HEAD_SIZE, :]
            k_scr[head, HEAD_SIZE:, :] = bias_rows
            v_scr[head] = half_with_one(slab_values, odd)


def place_queries(q_ref, q_scr, first):
    rows = q_ref.shape[0]
    stride = q_scr.shape[1] // 2
    for pair in range(q_scr.shape[0]):
        slab = q_ref[:, pair * LANES : (pair + 1) * LANES].astype(jnp.float32) * (
            1.0 / math.sqrt(HEAD_SIZE)
        )
        for odd in range(2):
            at = odd * stride + first
            q_scr[pair, at : at + rows, :] = half_with_one(slab, odd)


def attend(q_scr, k_scr, v_scr, s_scr, store, after_step):
    pairs = q_scr.shape[0]
    rows = q_scr.shape[1] // 2
    group = pairs // KEY_VALUE_HEADS

    def scores(pair, slot):
        head = lax.div(pair, group)
        s_scr[slot] = jnp.dot(q_scr[pair], k_scr[head], preferred_element_type=jnp.float32)

    def finish(pair, slot):
        head = lax.div(pair, group)
        s = s_scr[slot]
        largest = jnp.max(s, axis=1, keepdims=True)
        p = jnp.exp(s - largest).astype(jnp.bfloat16)
        summed = jnp.dot(p, v_scr[head], preferred_element_type=jnp.float32)
        total = summed[:, HEAD_SIZE : HEAD_SIZE + 1]
        mean = summed / total
        lse = jnp.broadcast_to(largest + jnp.log(total), mean.shape)
        low = lane_index((rows, LANES)) < HEAD_SIZE
        store(
            pair,
            jnp.where(low, mean[:rows], pltpu.roll(mean[rows:], HEAD_SIZE, 1)),
            jnp.where(low, lse[:rows], lse[rows:]),
        )

    scores(0, 0)

    def step(j, unused):
        scores(2 * j + 1, 1)
        finish(2 * j, 0)
        scores(jnp.minimum(2 * j + 2, pairs - 1), 0)
        finish(2 * j + 1, 1)
        after_step(j)
        return unused

    lax.fori_loop(0, pairs // 2, step, 0)


def attention_kernel(
    start_ref, length_ref, q_ref, cache_ref, rows_ref, marked_ref, out_ref, lse_ref,
    q_scr, k_scr, v_scr, s_scr,
):
    place_keys(start_ref, length_ref, cache_ref, rows_ref, marked_ref, k_scr, v_scr)
    place_queries(q_ref, q_scr, 0)

    def store(pair, mean, lse):
        out_ref[pair] = mean.astype(jnp.bfloat16)
        lse_ref[pair] = lse

    attend(q_scr, k_scr, v_scr, s_scr, store, lambda j: None)


def attention(queries, cache, row_key_value, start, length, marked):
    rows, width = queries.shape
    pairs = width // LANES
    keys = -(-(cache.shape[0] + row_key_value.shape[0]) // LANES) * LANES
    vmem = pl.BlockSpec(memory_space=pltpu.VMEM)
    smem = pl.BlockSpec(memory_space=pltpu.SMEM)
    return pl.pallas_call(
        attention_kernel,
        out_shape=(
            jax.ShapeDtypeStruct((pairs, rows, LANES), jnp.bfloat16),
            jax.ShapeDtypeStruct((pairs, rows, LANES), jnp.float32),
        ),
        in_specs=[smem, smem, vmem, vmem, vmem, vmem],
        out_specs=(vmem, vmem),
        scratch_shapes=[
            pltpu.VMEM((pairs, 2 * rows, LANES), jnp.bfloat16),
            pltpu.VMEM((KEY_VALUE_HEADS, LANES, keys), jnp.bfloat16),
            pltpu.VMEM((KEY_VALUE_HEADS, keys, LANES), jnp.bfloat16),
            pltpu.VMEM((2, 2 * rows, keys), jnp.float32),
        ],
        compiler_params=pltpu.CompilerParams(vmem_limit_bytes=40 * 1024 * 1024),
        cost_estimate=pl.CostEstimate(
            flops=4 * rows * width * keys,
            bytes_accessed=2 * cache.size + 8 * rows * width,
            transcendentals=rows * keys * width // HEAD_SIZE,
        ),
        name="attention",
    )(start, length, queries, cache, row_key_value, marked)


def chip_at(place, chips):
    return jnp.where(place < chips // 2, 2 * place, 2 * (chips - 1 - place) + 1)


def place_of(chip, chips):
    return jnp.where(chip % 2 == 0, chip // 2, chips - 1 - chip // 2)


def experts_kernel(
    devices, start_ref, length_ref, q_ref, cache_ref, rows_ref, marked_ref,
    resid_ref, gain_ref, shares_ref, gate_hbm, up_hbm, down_hbm, out_ref,
    q_scr, k_scr, v_scr, s_scr, visitor, own_mean, own_lse, host_mean, host_lse,
    far_mean, far_lse, residual,
    visit_sem, mean_send, mean_recv, lse_send, lse_recv,
    x, o, sibling_sums, ring_sums, hidden, w_gate, w_up, w_down,
    weight_sem, gather_send, gather_recv, share_send, share_recv,
    pair_send, pair_recv, ring_send, ring_recv,
):
    rows, half = q_ref.shape[0], q_ref.shape[0] // 2
    model = out_ref.shape[1]
    ff = w_down.shape[0]
    chips = devices // 2
    hops = chips // 2
    me = lax.axis_index("wide")
    core = me % 2
    place = place_of(me // 2, chips)
    sibling = me + 1 - 2 * core
    right = 2 * chip_at((place + 1) % chips, chips) + core
    left = 2 * chip_at((place + chips - 1) % chips, chips) + core

    def remote(source, target, send, recv, device):
        return pltpu.make_async_remote_copy(
            src_ref=source, dst_ref=target, send_sem=send, recv_sem=recv,
            device_id={"wide": device}, device_id_type=pl.DeviceIdType.MESH,
        )

    parts = (pl.ds(0, model // 2), pl.ds(model // 2, model // 2))
    wide_parts = (pl.ds(0, model // 2), pl.ds(model // 2, x.shape[2] - model // 2))

    loads = [
        pltpu.make_async_copy(source.at[0], target, weight_sem.at[i])
        for i, (source, target) in enumerate(
            ((gate_hbm, w_gate), (up_hbm, w_up), (down_hbm, w_down))
        )
    ]
    for load in loads:
        load.start()
    x[0, :rows, model:] = shares_ref[...]
    ring_sums[hops - 1, half : rows + half] = jnp.zeros((rows, model), jnp.bfloat16)

    barrier = pltpu.get_barrier_semaphore()
    for neighbour in (left, right, sibling):
        pl.semaphore_signal(
            barrier, inc=1, device_id={"wide": neighbour}, device_id_type=pl.DeviceIdType.MESH
        )
    pl.semaphore_wait(barrier, 3)

    visit = remote(q_ref, visitor, visit_sem.at[0], visit_sem.at[1], sibling)
    visit.start()
    place_keys(start_ref, length_ref, cache_ref, rows_ref, marked_ref, k_scr, v_scr)
    place_queries(q_ref, q_scr, 0)
    visit.wait_recv()
    place_queries(visitor, q_scr, rows)

    def store(pair, mean, lse):
        own_mean[pair] = mean[:rows]
        own_lse[pair] = lse[:rows]
        host_mean[pair] = mean[rows:].astype(jnp.bfloat16)
        host_lse[pair] = lse[rows:]

    def returned(j):
        two = pl.ds(2 * j, 2)
        return (
            remote(host_mean.at[two], far_mean.at[two], mean_send.at[j], mean_recv.at[j], sibling),
            remote(host_lse.at[two], far_lse.at[two], lse_send.at[j], lse_recv.at[j], sibling),
        )

    def send_back(j):
        for copy in returned(j):
            copy.start()

    attend(q_scr, k_scr, v_scr, s_scr, store, send_back)

    pairs = q_scr.shape[0]
    squares = jnp.zeros((rows, LANES), jnp.float32)
    for pair in range(pairs):
        if pair % 2 == 0:
            for copy in returned(pair // 2):
                copy.wait_recv()
        columns = slice(pair * LANES, (pair + 1) * LANES)
        near = own_mean[pair]
        far_part = 1.0 / (1.0 + jnp.exp(own_lse[pair] - far_lse[pair]))
        merged = near + (far_mean[pair].astype(jnp.float32) - near) * far_part
        total = resid_ref[:, columns].astype(jnp.float32) + merged.astype(jnp.bfloat16).astype(
            jnp.float32
        )
        residual[:, columns] = total
        squares = squares + total * total
    mean_square = jnp.sum(squares, axis=1, keepdims=True) / model
    x[0, :rows, :model] = (
        residual[...] * lax.rsqrt(mean_square + 1e-06) * gain_ref[...]
    ).astype(jnp.bfloat16)

    def gather(hop, part):
        if isinstance(hop, int) and hop == hops:
            top, bottom = pl.ds(0, half), pl.ds(half, half)
            from_left, from_right = top, bottom if hop == 1 else pl.ds(rows + half, half)
        else:
            top = bottom = None
            from_left, from_right = pl.ds(0, rows), pl.ds(rows, rows)
            if isinstance(hop, int) and hop == 1:
                from_right = pl.ds(0, rows)
        to_left = pl.ds(0, rows) if top is None else top
        to_right = pl.ds(rows, rows) if bottom is None else bottom
        columns = wide_parts[part]
        return (
            remote(x.at[hop - 1, from_left, columns], x.at[hop, to_left, columns],
                   gather_send.at[0, part, hop], gather_recv.at[0, part, hop], right),
            remote(x.at[hop - 1, from_right, columns], x.at[hop, to_right, columns],
                   gather_send.at[1, part, hop], gather_recv.at[1, part, hop], left),
        )

    def share(hop, count, part):
        return remote(x.at[hop, pl.ds(0, count), wide_parts[part]],
                      x.at[hop, pl.ds(count, count), wide_parts[part]],
                      share_send.at[part, hop], share_recv.at[part, hop], sibling)

    def pair(hop, count, part):
        return remote(o.at[hop, pl.ds(count, count), parts[part]],
                      sibling_sums.at[hop, pl.ds(0, count), parts[part]],
                      pair_send.at[part, hop], pair_recv.at[part, hop], sibling)

    def ring(hop, part):
        if isinstance(hop, int) and hop == hops:
            go_left = land_left = pl.ds(0, half)
            go_right, land_right = pl.ds(half, half), pl.ds(rows + half, half)
        else:
            go_left = land_left = pl.ds(0, rows)
            go_right = land_right = pl.ds(rows, rows)
        columns = parts[part]
        return (
            remote(o.at[hop, go_left, columns], ring_sums.at[hop - 1, land_left, columns],
                   ring_send.at[0, part, hop], ring_recv.at[0, part, hop], left),
            remote(o.at[hop, go_right, columns], ring_sums.at[hop - 1, land_right, columns],
                   ring_send.at[1, part, hop], ring_recv.at[1, part, hop], right),
        )

    def chunk_of(size):
        return next(c for c in (256, 128, size) if size % c == 0)

    def run_experts(hop, count):
        tail = x[hop, :count, model:].astype(jnp.float32)
        lane = lane_index(tail.shape)
        weight = jnp.sum(
            jnp.where((lane == me) | (lane == devices + me), tail, 0.0), axis=1, keepdims=True
        )
        step = chunk_of(ff)

        def hide(i, unused):
            columns = pl.ds(pl.multiple_of(i * step, step), step)
            rows_in = x[hop, :count, :model]
            g = jnp.dot(rows_in, w_gate[:, columns], preferred_element_type=jnp.float32)
            u = jnp.dot(rows_in, w_up[:, columns], preferred_element_type=jnp.float32)
            hidden[:count, columns] = (g / (1.0 + jnp.exp(-g)) * u).astype(jnp.bfloat16)
            return unused

        lax.fori_loop(0, ff // step, hide, 0, unroll=True)
        wide = chunk_of(model // 2)

        for part in range(2):

            def expand(i, unused):
                first_column = part * (model // 2) + i * wide
                columns = pl.ds(pl.multiple_of(first_column, wide), wide)
                y = jnp.dot(
                    hidden[:count], w_down[:, columns], preferred_element_type=jnp.float32
                )
                o[hop, :count, columns] = (y * weight).astype(jnp.bfloat16)
                return unused

            lax.fori_loop(0, model // 2 // wide, expand, 0, unroll=True)
            pair(hop, count // 2, part).start()

    def arrive(hop, count, onward):
        for part in range(2):
            coming = gather(hop, part)
            going = (None, None) if onward is None else gather(onward, part)
            for come, go in zip(coming, going):
                come.wait_recv()
                if go is not None:
                    go.start()
            share(hop, count, part).start()
        for part in range(2):
            share(hop, count, part).wait_recv()
        run_experts(hop, 2 * count)

    for part in range(2):
        for copy in gather(1, part):
            copy.start()
    for part in range(2):
        share(0, rows, part).start()
    for load in loads:
        load.wait()
    for part in range(2):
        share(0, rows, part).wait_recv()
    run_experts(0, 2 * rows)

    def middle(hop, unused):
        arrive(hop, 2 * rows, hop + 1)
        return unused

    lax.fori_loop(1, hops - 1, middle, 0)
    if hops > 1:
        arrive(hops - 1, 2 * rows, hops)
    arrive(hops, rows, None)

    def wider(ref, hop, some, columns):
        return ref[hop, some, columns].astype(jnp.float32)

    for part, columns in enumerate(parts):
        pair(hops, rows, part).wait_recv()
        some = pl.ds(0, rows)
        o[hops, some, columns] = (
            wider(o, hops, some, columns) + wider(sibling_sums, hops, some, columns)
        ).astype(jnp.bfloat16)
        for copy in ring(hops, part):
            copy.start()

    def add_up(hop):
        further = hops if isinstance(hop, int) and hop == hops - 1 else hop + 1
        for part, columns in enumerate(parts):
            pair(hop, 2 * rows, part).wait_recv()
            for side, (come, go) in enumerate(zip(ring(further, part), ring(hop, part))):
                come.wait_recv()
                some = pl.ds(side * rows, rows)
                o[hop, some, columns] = (
                    wider(o, hop, some, columns)
                    + wider(sibling_sums, hop, some, columns)
                    + wider(ring_sums, hop, some, columns)
                ).astype(jnp.bfloat16)
                go.start()

    if hops > 1:
        add_up(hops - 1)

    def nearer(i, unused):
        add_up(hops - 2 - i)
        return unused

    lax.fori_loop(0, hops - 2, nearer, 0)
    for part, columns in enumerate(parts):
        pair(0, rows, part).wait_recv()
        for copy in ring(1, part):
            copy.wait_recv()
        some, rest = pl.ds(0, rows), pl.ds(rows, rows)
        out_ref[:, columns] = (
            residual[:, columns]
            + wider(o, 0, some, columns)
            + wider(sibling_sums, 0, some, columns)
            + wider(ring_sums, 0, some, columns)
            + wider(ring_sums, 0, rest, columns)
        ).astype(out_ref.dtype)

    def sent(hop, count):
        for part in range(2):
            for copy in gather(hop, part) + ring(hop, part):
                copy.wait_send()
            share(hop, count, part).wait_send()
            pair(hop, count, part).wait_send()

    visit.wait_send()

    def drained(j, unused):
        for copy in returned(j):
            copy.wait_send()
        return unused

    lax.fori_loop(0, pairs // 2, drained, 0)
    for part in range(2):
        share(0, rows, part).wait_send()
        pair(0, rows, part).wait_send()
    if hops > 1:
        sent(1, 2 * rows)

    def drain(hop, unused):
        sent(hop, 2 * rows)
        return unused

    lax.fori_loop(2, hops, drain, 0)
    sent(hops, rows)


def scratch_of(rows, wide, model, ff, devices):
    hops = devices // 4
    return [
        ((hops + 1, 4 * rows, wide), jnp.bfloat16),
        ((hops + 1, 4 * rows, model), jnp.bfloat16),
        ((hops + 1, 2 * rows, model), jnp.bfloat16),
        ((hops, 2 * rows, model), jnp.bfloat16),
        ((4 * rows, ff), jnp.bfloat16),
        ((model, ff), jnp.bfloat16),
        ((model, ff), jnp.bfloat16),
        ((ff, model), jnp.bfloat16),
    ]


def fits(buffers):
    return sum(2 * math.prod(shape) for shape, unused in buffers) < 32 * 1024 * 1024


def whole_layer(
    start, length, queries, cache, row_key_value, marked, resid, gain, shares,
    w_gate, w_up, w_down, devices,
):
    rows = queries.shape[0]
    model, ff = w_gate.shape[1:]
    wide = model + shares.shape[1]
    hops = devices // 4
    pairs = queries.shape[1] // LANES
    keys = -(-(cache.shape[0] + rows) // LANES) * LANES
    anywhere = pl.BlockSpec(memory_space=pl.ANY)
    vmem = pl.BlockSpec(memory_space=pltpu.VMEM)
    smem = pl.BlockSpec(memory_space=pltpu.SMEM)
    dma = pltpu.SemaphoreType.DMA
    half_doc = (pairs, rows, LANES)
    return pl.pallas_call(
        functools.partial(experts_kernel, devices),
        out_shape=jax.ShapeDtypeStruct((rows, model), jnp.bfloat16),
        in_specs=[smem, smem] + [vmem] * 7 + [anywhere] * 3,
        out_specs=vmem,
        scratch_shapes=[
            pltpu.VMEM((pairs, 4 * rows, LANES), jnp.bfloat16),
            pltpu.VMEM((KEY_VALUE_HEADS, LANES, keys), jnp.bfloat16),
            pltpu.VMEM((KEY_VALUE_HEADS, keys, LANES), jnp.bfloat16),
            pltpu.VMEM((2, 4 * rows, keys), jnp.float32),
            pltpu.VMEM((rows, queries.shape[1]), jnp.bfloat16),
            pltpu.VMEM(half_doc, jnp.float32),
            pltpu.VMEM(half_doc, jnp.float32),
            pltpu.VMEM(half_doc, jnp.bfloat16),
            pltpu.VMEM(half_doc, jnp.float32),
            pltpu.VMEM(half_doc, jnp.bfloat16),
            pltpu.VMEM(half_doc, jnp.float32),
            pltpu.VMEM((rows, model), jnp.float32),
            dma((2,)),
        ]
        + [dma((pairs // 2,))] * 4
        + [
            pltpu.VMEM(shape, kind)
            for shape, kind in scratch_of(rows, wide, model, ff, devices)
        ]
        + [dma((3,))]
        + [dma((2, 2, hops + 1)), dma((2, 2, hops + 1)), dma((2, hops + 1)), dma((2, hops + 1))]
        + [dma((2, hops + 1)), dma((2, hops + 1)), dma((2, 2, hops + 1)), dma((2, 2, hops + 1))],
        compiler_params=pltpu.CompilerParams(
            collective_id=0, has_side_effects=True, vmem_limit_bytes=58 * 1024 * 1024
        ),
        cost_estimate=pl.CostEstimate(
            flops=6 * rows * devices * model * ff + 8 * rows * model * keys,
            bytes_accessed=6 * model * ff + 2 * cache.size,
            transcendentals=rows * devices * ff,
        ),
        name="whole_layer",
    )(
        start, length, queries, cache, row_key_value, marked, resid, gain, shares,
        w_gate, w_up, w_down,
    )


def local(
    query_rows,
    row_key_value,
    key_value_cache,
    resid,
    norm_gain,
    lengths,
    positions,
    expert_ids,
    gate_scores,
    w_gate,
    w_up,
    w_down,
):
    rows = query_rows.shape[0]
    width = query_rows.shape[1]
    span = key_value_cache.shape[0]
    device = lax.axis_index("wide")
    experts = lax.axis_size("wide")
    doc_index = device // 2
    half_index = device % 2

    mix = gate_scores / jnp.sum(gate_scores, axis=-1, keepdims=True)
    chosen = expert_ids[..., None] == jnp.arange(experts, dtype=jnp.int32)
    share = jnp.sum(jnp.where(chosen, mix[..., None], 0.0), axis=1)
    high = share.astype(jnp.bfloat16)
    low = (share - high.astype(jnp.float32)).astype(jnp.bfloat16)
    spare = -(2 * experts) % LANES
    shares = jnp.concatenate([high, low, jnp.zeros((rows, spare), jnp.bfloat16)], axis=1)

    length = lax.dynamic_slice_in_dim(lengths, doc_index, 1, 0)
    marked = lax.dynamic_index_in_dim(positions, doc_index, 0, keepdims=False)[:, None]
    start = jnp.reshape(half_index * span, (1,)).astype(jnp.int32)
    model, ff = w_gate.shape[1:]
    if experts % 4 == 0 and fits(scratch_of(rows, model + shares.shape[1], model, ff, experts)):
        return whole_layer(
            start, length, query_rows, key_value_cache, row_key_value, marked, resid,
            norm_gain[None, :], shares, w_gate, w_up, w_down, experts,
        )

    visitor = swapped(query_rows, "wide", 0)
    means, lse = attention(
        jnp.concatenate([query_rows, visitor], axis=0),
        key_value_cache, row_key_value, start, length, marked,
    )
    far_mean = swapped(means[:, rows:], "wide", 0).astype(jnp.float32)
    far_lse = swapped(lse[:, rows:], "wide", 0)
    own_mean = means[:, :rows].astype(jnp.float32)
    own_lse = lse[:, :rows]
    far_part = 1.0 / (1.0 + jnp.exp(own_lse - far_lse))
    merged = own_mean + (far_mean - own_mean) * far_part
    attended = jnp.swapaxes(merged, 0, 1).reshape(rows, width).astype(jnp.bfloat16)

    residual = resid.astype(jnp.float32) + attended.astype(jnp.float32)
    normed = (
        residual
        * lax.rsqrt(jnp.mean(residual * residual, axis=-1, keepdims=True) + 1e-06)
        * norm_gain
    ).astype(jnp.bfloat16)

    first = jnp.concatenate([normed, shares], axis=1)

    gathered = lax.all_gather(first, "wide", axis=0, tiled=True)
    everyone = gathered[:, :model]
    weight = sum(
        lax.dynamic_slice_in_dim(gathered, model + device + part * experts, 1, 1).astype(
            jnp.float32
        )
        for part in range(2)
    )
    gate_act = jnp.dot(everyone, w_gate[0], preferred_element_type=jnp.float32)
    up_act = jnp.dot(everyone, w_up[0], preferred_element_type=jnp.float32)
    hidden = (jax.nn.silu(gate_act) * up_act).astype(jnp.bfloat16)
    expert_out = jnp.dot(hidden, w_down[0], preferred_element_type=jnp.float32)
    weighted = (expert_out * weight).astype(jnp.bfloat16)
    routed = lax.psum_scatter(weighted, "wide", scatter_dimension=0, tiled=True)
    return (residual + routed.astype(jnp.float32)).astype(jnp.bfloat16)


def solution(mesh):
    return jax.shard_map(
        local,
        mesh=mesh,
        in_specs=(
            P(("grp", "wide"), None),
            P(("grp", "wide"), None),
            P(("grp", "wide"), None),
            P(("grp", "wide"), None),
            P(),
            P("grp"),
            P("grp", None),
            P(("grp", "wide"), None),
            P(("grp", "wide"), None),
            P("wide", None, None),
            P("wide", None, None),
            P("wide", None, None),
        ),
        out_specs=P(("grp", "wide"), None),
        check_vma=False,
    )
```

```python
import functools
import math

import jax
import jax.numpy as jnp
from jax import lax
from jax.experimental import pallas as pl
from jax.experimental.pallas import tpu as pltpu
from jax.sharding import PartitionSpec as P

KEY_VALUE_HEADS = 4
HEAD_SIZE = 64
LANES = 128
NEVER = -1e30


def swapped(shard, axis, bit):
    return lax.ppermute(shard, axis, [(i, i ^ 1 << bit) for i in range(lax.axis_size(axis))])


def lane_index(shape):
    return lax.broadcasted_iota(jnp.int32, shape, 1)


def half_with_one(slab, odd):
    values = slab.astype(jnp.float32)
    if odd:
        values = pltpu.roll(values, HEAD_SIZE, 1)
    lane = lane_index(values.shape)
    return jnp.where(
        lane < HEAD_SIZE, values, jnp.where(lane == HEAD_SIZE, 1.0, 0.0)
    ).astype(jnp.bfloat16)


def place_keys(start, length, cache_ref, rows_ref, marked, k_scr, v_scr):
    span = cache_ref.shape[0]
    own = rows_ref.shape[0]
    keys = k_scr.shape[2]
    width = KEY_VALUE_HEADS * HEAD_SIZE

    location = lane_index((1, keys))
    place = start + location
    hit = jnp.max(
        jnp.where(marked == place.astype(jnp.float32), 1.0, 0.0), axis=0, keepdims=True
    )
    in_cache = (place < length) & (hit == 0.0) & (location < span)
    usable = in_cache | ((location >= span) & (location < span + own))
    bias = jnp.where(usable, 0.0, NEVER)
    row = lax.broadcasted_iota(jnp.int32, (HEAD_SIZE, keys), 0)
    bias_rows = jnp.where(row == 0, bias, 0.0).astype(jnp.bfloat16)
    pad = keys - span - own
    for slab in range(KEY_VALUE_HEADS // 2):
        columns = slice(slab * LANES, (slab + 1) * LANES)
        value_columns = slice(width + slab * LANES, width + (slab + 1) * LANES)
        tail = [rows_ref[:, columns]]
        value_tail = [rows_ref[:, value_columns]]
        if pad:
            tail.append(jnp.zeros((pad, LANES), jnp.bfloat16))
            value_tail.append(jnp.zeros((pad, LANES), jnp.bfloat16))
        slab_keys = jnp.concatenate([cache_ref[:, columns]] + tail, axis=0).T
        slab_values = jnp.concatenate([cache_ref[:, value_columns]] + value_tail, axis=0)
        for odd in range(2):
            head = 2 * slab + odd
            k_scr[head, :HEAD_SIZE, :] = slab_keys[odd * HEAD_SIZE : (odd + 1) * HEAD_SIZE, :]
            k_scr[head, HEAD_SIZE:, :] = bias_rows
            v_scr[head] = half_with_one(slab_values, odd)


def place_queries(q_ref, q_scr, first):
    rows = q_ref.shape[0]
    pairs = q_ref.shape[1] // LANES
    joined = pairs // q_scr.shape[0]
    stride = q_scr.shape[1] // (2 * joined)
    for pair in range(pairs):
        slab = q_ref[:, pair * LANES : (pair + 1) * LANES].astype(jnp.float32) * (
            1.0 / math.sqrt(HEAD_SIZE)
        )
        for odd in range(2):
            at = (2 * (pair % joined) + odd) * stride + first
            q_scr[pair // joined, at : at + rows, :] = half_with_one(slab, odd)


def attend(q_scr, k_scr, v_scr, s_scr, joined, store, after_step):
    steps = q_scr.shape[0]
    rows = q_scr.shape[1] // (2 * joined)
    group = steps // KEY_VALUE_HEADS

    def scores(step, slot):
        head = lax.div(step, group)
        s_scr[slot] = jnp.dot(q_scr[step], k_scr[head], preferred_element_type=jnp.float32)

    def finish(step, slot):
        head = lax.div(step, group)
        s = s_scr[slot]
        largest = jnp.max(s, axis=1, keepdims=True)
        p = jnp.exp(s - largest).astype(jnp.bfloat16)
        summed = jnp.dot(p, v_scr[head], preferred_element_type=jnp.float32)
        total = summed[:, HEAD_SIZE : HEAD_SIZE + 1]
        mean = summed / total
        lse = jnp.broadcast_to(largest + jnp.log(total), mean.shape)
        low = lane_index((rows, LANES)) < HEAD_SIZE
        for i in range(joined):
            even = slice(2 * i * rows, (2 * i + 1) * rows)
            odd = slice((2 * i + 1) * rows, (2 * i + 2) * rows)
            store(
                step * joined + i,
                jnp.where(low, mean[even], pltpu.roll(mean[odd], HEAD_SIZE, 1)),
                jnp.where(low, lse[even], lse[odd]),
            )

    scores(0, 0)

    def two_steps(j, unused):
        scores(2 * j + 1, 1)
        finish(2 * j, 0)
        scores(jnp.minimum(2 * j + 2, steps - 1), 0)
        finish(2 * j + 1, 1)
        after_step(j)
        return unused

    lax.fori_loop(0, steps // 2, two_steps, 0)


def attention_kernel(
    start_ref, length_ref, q_ref, cache_ref, rows_ref, marked_ref, out_ref, lse_ref,
    q_scr, k_scr, v_scr, s_scr,
):
    place_keys(
        start_ref[0], length_ref[0], cache_ref, rows_ref,
        marked_ref[...].astype(jnp.float32), k_scr, v_scr,
    )
    place_queries(q_ref, q_scr, 0)

    def store(pair, mean, lse):
        out_ref[pair] = mean.astype(jnp.bfloat16)
        lse_ref[pair] = lse

    attend(q_scr, k_scr, v_scr, s_scr, 1, store, lambda j: None)


def attention(queries, cache, row_key_value, start, length, marked):
    rows, width = queries.shape
    pairs = width // LANES
    keys = -(-(cache.shape[0] + row_key_value.shape[0]) // LANES) * LANES
    vmem = pl.BlockSpec(memory_space=pltpu.VMEM)
    smem = pl.BlockSpec(memory_space=pltpu.SMEM)
    return pl.pallas_call(
        attention_kernel,
        out_shape=(
            jax.ShapeDtypeStruct((pairs, rows, LANES), jnp.bfloat16),
            jax.ShapeDtypeStruct((pairs, rows, LANES), jnp.float32),
        ),
        in_specs=[smem, smem, vmem, vmem, vmem, vmem],
        out_specs=(vmem, vmem),
        scratch_shapes=[
            pltpu.VMEM((pairs, 2 * rows, LANES), jnp.bfloat16),
            pltpu.VMEM((KEY_VALUE_HEADS, LANES, keys), jnp.bfloat16),
            pltpu.VMEM((KEY_VALUE_HEADS, keys, LANES), jnp.bfloat16),
            pltpu.VMEM((2, 2 * rows, keys), jnp.float32),
        ],
        compiler_params=pltpu.CompilerParams(vmem_limit_bytes=40 * 1024 * 1024),
        cost_estimate=pl.CostEstimate(
            flops=4 * rows * width * keys,
            bytes_accessed=2 * cache.size + 8 * rows * width,
            transcendentals=rows * keys * width // HEAD_SIZE,
        ),
        name="attention",
    )(start, length, queries, cache, row_key_value, marked)


def chip_at(place, chips):
    return jnp.where(place < chips // 2, 2 * place, 2 * (chips - 1 - place) + 1)


def place_of(chip, chips):
    return jnp.where(chip % 2 == 0, chip // 2, chips - 1 - chip // 2)


def experts_kernel(
    devices, joined, lengths_ref, q_ref, cache_ref, rows_ref, positions_ref,
    resid_ref, gain_ref, ids_ref, gates_ref, gate_hbm, up_hbm, down_hbm, out_ref,
    q_scr, k_scr, v_scr, s_scr, visitor, own_mean, own_lse, host_mean, host_lse,
    far_mean, far_lse, residual,
    visit_sem, mean_send, mean_recv, lse_send, lse_recv,
    x, o, sibling_sums, ring_sums, hidden, w_gate, w_up, w_down,
    weight_sem, gather_send, gather_recv, share_send, share_recv,
    pair_send, pair_recv, ring_send, ring_recv,
):
    rows, half = q_ref.shape[0], q_ref.shape[0] // 2
    model = out_ref.shape[1]
    ff = w_down.shape[0]
    chips = devices // 2
    hops = chips // 2
    me = lax.axis_index("wide")
    core = me % 2
    place = place_of(me // 2, chips)
    sibling = me + 1 - 2 * core
    right = 2 * chip_at((place + 1) % chips, chips) + core
    left = 2 * chip_at((place + chips - 1) % chips, chips) + core

    def remote(source, target, send, recv, device):
        return pltpu.make_async_remote_copy(
            src_ref=source, dst_ref=target, send_sem=send, recv_sem=recv,
            device_id={"wide": device}, device_id_type=pl.DeviceIdType.MESH,
        )

    parts = (pl.ds(0, model // 2), pl.ds(model // 2, model // 2))
    wide_parts = (pl.ds(0, model // 2), pl.ds(model // 2, x.shape[2] - model // 2))

    loads = [
        pltpu.make_async_copy(source.at[0], target, weight_sem.at[i])
        for i, (source, target) in enumerate(
            ((gate_hbm, w_gate), (up_hbm, w_up), (down_hbm, w_down))
        )
    ]
    for load in loads:
        load.start()
    gates = gates_ref[...]
    mix = gates / jnp.sum(gates, axis=1, keepdims=True)
    lane = lane_index((rows, x.shape[2] - model))
    high = jnp.zeros(lane.shape, jnp.float32)
    low = jnp.zeros(lane.shape, jnp.float32)
    for choice in range(ids_ref.shape[1]):
        expert, amount = ids_ref[:, choice : choice + 1], mix[:, choice : choice + 1]
        high = high + jnp.where(lane == expert, amount, 0.0)
        low = low + jnp.where(lane == expert + devices, amount, 0.0)
    low = low - low.astype(jnp.bfloat16).astype(jnp.float32)
    x[0, :rows, model:] = (high + low).astype(jnp.bfloat16)
    ring_sums[hops - 1, half : rows + half] = jnp.zeros((rows, model), jnp.bfloat16)

    barrier = pltpu.get_barrier_semaphore()
    for neighbour in (left, right, sibling):
        pl.semaphore_signal(
            barrier, inc=1, device_id={"wide": neighbour}, device_id_type=pl.DeviceIdType.MESH
        )
    pl.semaphore_wait(barrier, 3)

    visit = remote(q_ref, visitor, visit_sem.at[0], visit_sem.at[1], sibling)
    visit.start()
    document = me // 2
    marked = positions_ref[pl.ds(document, 1), :].astype(jnp.float32)
    marked = jnp.broadcast_to(marked, (LANES, marked.shape[1])).T[:, :1]
    place_keys(
        core * cache_ref.shape[0], lengths_ref[document], cache_ref, rows_ref, marked,
        k_scr, v_scr,
    )
    place_queries(q_ref, q_scr, 0)
    visit.wait_recv()
    place_queries(visitor, q_scr, rows)

    def store(pair, mean, lse):
        own_mean[pair] = mean[:rows]
        own_lse[pair] = lse[:rows]
        host_mean[pair] = mean[rows:].astype(jnp.bfloat16)
        host_lse[pair] = lse[rows:]

    def returned(j):
        two = pl.ds(2 * joined * j, 2 * joined)
        return (
            remote(host_mean.at[two], far_mean.at[two], mean_send.at[j], mean_recv.at[j], sibling),
            remote(host_lse.at[two], far_lse.at[two], lse_send.at[j], lse_recv.at[j], sibling),
        )

    def send_back(j):
        for copy in returned(j):
            copy.start()

    attend(q_scr, k_scr, v_scr, s_scr, joined, store, send_back)

    pairs = own_mean.shape[0]
    squares = jnp.zeros((rows, LANES), jnp.float32)
    for pair in range(pairs):
        if pair % (2 * joined) == 0:
            for copy in returned(pair // (2 * joined)):
                copy.wait_recv()
        columns = slice(pair * LANES, (pair + 1) * LANES)
        near = own_mean[pair]
        far_part = 1.0 / (1.0 + jnp.exp(own_lse[pair] - far_lse[pair]))
        merged = near + (far_mean[pair].astype(jnp.float32) - near) * far_part
        total = resid_ref[:, columns].astype(jnp.float32) + merged.astype(jnp.bfloat16).astype(
            jnp.float32
        )
        residual[:, columns] = total
        squares = squares + total * total
    mean_square = jnp.sum(squares, axis=1, keepdims=True) / model
    x[0, :rows, :model] = (
        residual[...] * lax.rsqrt(mean_square + 1e-06) * gain_ref[...]
    ).astype(jnp.bfloat16)

    def gather(hop, part):
        if isinstance(hop, int) and hop == hops:
            top, bottom = pl.ds(0, half), pl.ds(half, half)
            from_left, from_right = top, bottom if hop == 1 else pl.ds(rows + half, half)
        else:
            top = bottom = None
            from_left, from_right = pl.ds(0, rows), pl.ds(rows, rows)
            if isinstance(hop, int) and hop == 1:
                from_right = pl.ds(0, rows)
        to_left = pl.ds(0, rows) if top is None else top
        to_right = pl.ds(rows, rows) if bottom is None else bottom
        columns = wide_parts[part]
        return (
            remote(x.at[hop - 1, from_left, columns], x.at[hop, to_left, columns],
                   gather_send.at[0, part, hop], gather_recv.at[0, part, hop], right),
            remote(x.at[hop - 1, from_right, columns], x.at[hop, to_right, columns],
                   gather_send.at[1, part, hop], gather_recv.at[1, part, hop], left),
        )

    def share(hop, count, part):
        return remote(x.at[hop, pl.ds(0, count), wide_parts[part]],
                      x.at[hop, pl.ds(count, count), wide_parts[part]],
                      share_send.at[part, hop], share_recv.at[part, hop], sibling)

    def pair(hop, count, part):
        return remote(o.at[hop, pl.ds(count, count), parts[part]],
                      sibling_sums.at[hop, pl.ds(0, count), parts[part]],
                      pair_send.at[part, hop], pair_recv.at[part, hop], sibling)

    def ring(hop, part):
        if isinstance(hop, int) and hop == hops:
            go_left = land_left = pl.ds(0, half)
            go_right, land_right = pl.ds(half, half), pl.ds(rows + half, half)
        else:
            go_left = land_left = pl.ds(0, rows)
            go_right = land_right = pl.ds(rows, rows)
        columns = parts[part]
        return (
            remote(o.at[hop, go_left, columns], ring_sums.at[hop - 1, land_left, columns],
                   ring_send.at[0, part, hop], ring_recv.at[0, part, hop], left),
            remote(o.at[hop, go_right, columns], ring_sums.at[hop - 1, land_right, columns],
                   ring_send.at[1, part, hop], ring_recv.at[1, part, hop], right),
        )

    def chunk_of(size):
        return next(c for c in (256, 128, size) if size % c == 0)

    def run_experts(hop, count):
        tail = x[hop, :count, model:].astype(jnp.float32)
        lane = lane_index(tail.shape)
        weight = jnp.sum(
            jnp.where((lane == me) | (lane == devices + me), tail, 0.0), axis=1, keepdims=True
        )
        step = chunk_of(ff)

        def hide(i, unused):
            columns = pl.ds(pl.multiple_of(i * step, step), step)
            rows_in = x[hop, :count, :model]
            g = jnp.dot(rows_in, w_gate[:, columns], preferred_element_type=jnp.float32)
            u = jnp.dot(rows_in, w_up[:, columns], preferred_element_type=jnp.float32)
            hidden[:count, columns] = (g / (1.0 + jnp.exp(-g)) * u).astype(jnp.bfloat16)
            return unused

        lax.fori_loop(0, ff // step, hide, 0, unroll=True)
        wide = chunk_of(model // 2)

        for part in range(2):

            def expand(i, unused):
                first_column = part * (model // 2) + i * wide
                columns = pl.ds(pl.multiple_of(first_column, wide), wide)
                y = jnp.dot(
                    hidden[:count], w_down[:, columns], preferred_element_type=jnp.float32
                )
                o[hop, :count, columns] = (y * weight).astype(jnp.bfloat16)
                return unused

            lax.fori_loop(0, model // 2 // wide, expand, 0, unroll=True)
            pair(hop, count // 2, part).start()

    def arrive(hop, count, onward):
        for part in range(2):
            coming = gather(hop, part)
            going = (None, None) if onward is None else gather(onward, part)
            for come, go in zip(coming, going):
                come.wait_recv()
                if go is not None:
                    go.start()
            share(hop, count, part).start()
        for part in range(2):
            share(hop, count, part).wait_recv()
        run_experts(hop, 2 * count)

    for part in range(2):
        for copy in gather(1, part):
            copy.start()
    for part in range(2):
        share(0, rows, part).start()
    for load in loads:
        load.wait()
    for part in range(2):
        share(0, rows, part).wait_recv()
    run_experts(0, 2 * rows)

    def middle(hop, unused):
        arrive(hop, 2 * rows, hop + 1)
        return unused

    lax.fori_loop(1, hops - 1, middle, 0)
    if hops > 1:
        arrive(hops - 1, 2 * rows, hops)
    arrive(hops, rows, None)

    def wider(ref, hop, some, columns):
        return ref[hop, some, columns].astype(jnp.float32)

    for part, columns in enumerate(parts):
        pair(hops, rows, part).wait_recv()
        some = pl.ds(0, rows)
        o[hops, some, columns] = (
            wider(o, hops, some, columns) + wider(sibling_sums, hops, some, columns)
        ).astype(jnp.bfloat16)
        for copy in ring(hops, part):
            copy.start()

    def add_up(hop):
        further = hops if isinstance(hop, int) and hop == hops - 1 else hop + 1
        for part, columns in enumerate(parts):
            pair(hop, 2 * rows, part).wait_recv()
            for side, (come, go) in enumerate(zip(ring(further, part), ring(hop, part))):
                come.wait_recv()
                some = pl.ds(side * rows, rows)
                o[hop, some, columns] = (
                    wider(o, hop, some, columns)
                    + wider(sibling_sums, hop, some, columns)
                    + wider(ring_sums, hop, some, columns)
                ).astype(jnp.bfloat16)
                go.start()

    if hops > 1:
        add_up(hops - 1)

    def nearer(i, unused):
        add_up(hops - 2 - i)
        return unused

    lax.fori_loop(0, hops - 2, nearer, 0)
    for part, columns in enumerate(parts):
        pair(0, rows, part).wait_recv()
        for copy in ring(1, part):
            copy.wait_recv()
        some, rest = pl.ds(0, rows), pl.ds(rows, rows)
        out_ref[:, columns] = (
            residual[:, columns]
            + wider(o, 0, some, columns)
            + wider(sibling_sums, 0, some, columns)
            + wider(ring_sums, 0, some, columns)
            + wider(ring_sums, 0, rest, columns)
        ).astype(out_ref.dtype)

    def sent(hop, count):
        for part in range(2):
            for copy in gather(hop, part) + ring(hop, part):
                copy.wait_send()
            share(hop, count, part).wait_send()
            pair(hop, count, part).wait_send()

    visit.wait_send()

    def drained(j, unused):
        for copy in returned(j):
            copy.wait_send()
        return unused

    lax.fori_loop(0, pairs // (2 * joined), drained, 0)
    for part in range(2):
        share(0, rows, part).wait_send()
        pair(0, rows, part).wait_send()
    if hops > 1:
        sent(1, 2 * rows)

    def drain(hop, unused):
        sent(hop, 2 * rows)
        return unused

    lax.fori_loop(2, hops, drain, 0)
    sent(hops, rows)


def scratch_of(rows, wide, model, ff, devices):
    hops = devices // 4
    return [
        ((hops + 1, 4 * rows, wide), jnp.bfloat16),
        ((hops + 1, 4 * rows, model), jnp.bfloat16),
        ((hops + 1, 2 * rows, model), jnp.bfloat16),
        ((hops, 2 * rows, model), jnp.bfloat16),
        ((4 * rows, ff), jnp.bfloat16),
        ((model, ff), jnp.bfloat16),
        ((model, ff), jnp.bfloat16),
        ((ff, model), jnp.bfloat16),
    ]


def fits(buffers):
    return sum(2 * math.prod(shape) for shape, unused in buffers) < 32 * 1024 * 1024


def share_width(devices):
    return -(-2 * devices // LANES) * LANES


def whole_layer(
    lengths, queries, cache, row_key_value, positions, resid, gain, ids, gates,
    w_gate, w_up, w_down, devices,
):
    rows = queries.shape[0]
    model, ff = w_gate.shape[1:]
    wide = model + share_width(devices)
    hops = devices // 4
    pairs = queries.shape[1] // LANES
    keys = -(-(cache.shape[0] + rows) // LANES) * LANES
    anywhere = pl.BlockSpec(memory_space=pl.ANY)
    vmem = pl.BlockSpec(memory_space=pltpu.VMEM)
    smem = pl.BlockSpec(memory_space=pltpu.SMEM)
    dma = pltpu.SemaphoreType.DMA
    half_doc = (pairs, rows, LANES)
    joined = 2 if pairs % (4 * KEY_VALUE_HEADS) == 0 else 1
    return pl.pallas_call(
        functools.partial(experts_kernel, devices, joined),
        out_shape=jax.ShapeDtypeStruct((rows, model), jnp.bfloat16),
        in_specs=[smem] + [vmem] * 8 + [anywhere] * 3,
        out_specs=vmem,
        scratch_shapes=[
            pltpu.VMEM((pairs // joined, 4 * joined * rows, LANES), jnp.bfloat16),
            pltpu.VMEM((KEY_VALUE_HEADS, LANES, keys), jnp.bfloat16),
            pltpu.VMEM((KEY_VALUE_HEADS, keys, LANES), jnp.bfloat16),
            pltpu.VMEM((2, 4 * joined * rows, keys), jnp.float32),
            pltpu.VMEM((rows, queries.shape[1]), jnp.bfloat16),
            pltpu.VMEM(half_doc, jnp.float32),
            pltpu.VMEM(half_doc, jnp.float32),
            pltpu.VMEM(half_doc, jnp.bfloat16),
            pltpu.VMEM(half_doc, jnp.float32),
            pltpu.VMEM(half_doc, jnp.bfloat16),
            pltpu.VMEM(half_doc, jnp.float32),
            pltpu.VMEM((rows, model), jnp.float32),
            dma((2,)),
        ]
        + [dma((pairs // (2 * joined),))] * 4
        + [
            pltpu.VMEM(shape, kind)
            for shape, kind in scratch_of(rows, wide, model, ff, devices)
        ]
        + [dma((3,))]
        + [dma((2, 2, hops + 1)), dma((2, 2, hops + 1)), dma((2, hops + 1)), dma((2, hops + 1))]
        + [dma((2, hops + 1)), dma((2, hops + 1)), dma((2, 2, hops + 1)), dma((2, 2, hops + 1))],
        compiler_params=pltpu.CompilerParams(
            collective_id=0, has_side_effects=True, vmem_limit_bytes=58 * 1024 * 1024
        ),
        cost_estimate=pl.CostEstimate(
            flops=6 * rows * devices * model * ff + 8 * rows * model * keys,
            bytes_accessed=6 * model * ff + 2 * cache.size,
            transcendentals=rows * devices * ff,
        ),
        name="whole_layer",
    )(
        lengths, queries, cache, row_key_value, positions, resid, gain, ids, gates,
        w_gate, w_up, w_down,
    )


def local(
    query_rows,
    row_key_value,
    key_value_cache,
    resid,
    norm_gain,
    lengths,
    positions,
    expert_ids,
    gate_scores,
    w_gate,
    w_up,
    w_down,
):
    rows = query_rows.shape[0]
    width = query_rows.shape[1]
    span = key_value_cache.shape[0]
    device = lax.axis_index("wide")
    experts = lax.axis_size("wide")
    doc_index = device // 2
    half_index = device % 2

    model, ff = w_gate.shape[1:]
    buffers = scratch_of(rows, model + share_width(experts), model, ff, experts)
    if experts % 4 == 0 and fits(buffers):
        return whole_layer(
            lengths, query_rows, key_value_cache, row_key_value, positions, resid,
            norm_gain[None, :], expert_ids, gate_scores, w_gate, w_up, w_down, experts,
        )

    mix = gate_scores / jnp.sum(gate_scores, axis=-1, keepdims=True)
    chosen = expert_ids[..., None] == jnp.arange(experts, dtype=jnp.int32)
    share = jnp.sum(jnp.where(chosen, mix[..., None], 0.0), axis=1)
    high = share.astype(jnp.bfloat16)
    low = (share - high.astype(jnp.float32)).astype(jnp.bfloat16)
    spare = -(2 * experts) % LANES
    shares = jnp.concatenate([high, low, jnp.zeros((rows, spare), jnp.bfloat16)], axis=1)

    length = lax.dynamic_slice_in_dim(lengths, doc_index, 1, 0)
    marked = lax.dynamic_index_in_dim(positions, doc_index, 0, keepdims=False)[:, None]
    start = jnp.reshape(half_index * span, (1,)).astype(jnp.int32)
    visitor = swapped(query_rows, "wide", 0)
    means, lse = attention(
        jnp.concatenate([query_rows, visitor], axis=0),
        key_value_cache, row_key_value, start, length, marked,
    )
    far_mean = swapped(means[:, rows:], "wide", 0).astype(jnp.float32)
    far_lse = swapped(lse[:, rows:], "wide", 0)
    own_mean = means[:, :rows].astype(jnp.float32)
    own_lse = lse[:, :rows]
    far_part = 1.0 / (1.0 + jnp.exp(own_lse - far_lse))
    merged = own_mean + (far_mean - own_mean) * far_part
    attended = jnp.swapaxes(merged, 0, 1).reshape(rows, width).astype(jnp.bfloat16)

    residual = resid.astype(jnp.float32) + attended.astype(jnp.float32)
    normed = (
        residual
        * lax.rsqrt(jnp.mean(residual * residual, axis=-1, keepdims=True) + 1e-06)
        * norm_gain
    ).astype(jnp.bfloat16)

    first = jnp.concatenate([normed, shares], axis=1)

    gathered = lax.all_gather(first, "wide", axis=0, tiled=True)
    everyone = gathered[:, :model]
    weight = sum(
        lax.dynamic_slice_in_dim(gathered, model + device + part * experts, 1, 1).astype(
            jnp.float32
        )
        for part in range(2)
    )
    gate_act = jnp.dot(everyone, w_gate[0], preferred_element_type=jnp.float32)
    up_act = jnp.dot(everyone, w_up[0], preferred_element_type=jnp.float32)
    hidden = (jax.nn.silu(gate_act) * up_act).astype(jnp.bfloat16)
    expert_out = jnp.dot(hidden, w_down[0], preferred_element_type=jnp.float32)
    weighted = (expert_out * weight).astype(jnp.bfloat16)
    routed = lax.psum_scatter(weighted, "wide", scatter_dimension=0, tiled=True)
    return (residual + routed.astype(jnp.float32)).astype(jnp.bfloat16)


def solution(mesh):
    return jax.shard_map(
        local,
        mesh=mesh,
        in_specs=(
            P(("grp", "wide"), None),
            P(("grp", "wide"), None),
            P(("grp", "wide"), None),
            P(("grp", "wide"), None),
            P(),
            P("grp"),
            P("grp", None),
            P(("grp", "wide"), None),
            P(("grp", "wide"), None),
            P("wide", None, None),
            P("wide", None, None),
            P("wide", None, None),
        ),
        out_specs=P(("grp", "wide"), None),
        check_vma=False,
    )
```

```python
import functools
import math

import jax
import jax.numpy as jnp
from jax import lax
from jax.experimental import pallas as pl
from jax.experimental.pallas import tpu as pltpu
from jax.sharding import PartitionSpec as P

KEY_VALUE_HEADS = 4
HEAD_SIZE = 64
LANES = 128
NEVER = -1e30


def swapped(shard, axis, bit):
    return lax.ppermute(shard, axis, [(i, i ^ 1 << bit) for i in range(lax.axis_size(axis))])


def lane_index(shape):
    return lax.broadcasted_iota(jnp.int32, shape, 1)


def half_with_one(slab, odd):
    values = slab.astype(jnp.float32)
    if odd:
        values = pltpu.roll(values, HEAD_SIZE, 1)
    lane = lane_index(values.shape)
    return jnp.where(
        lane < HEAD_SIZE, values, jnp.where(lane == HEAD_SIZE, 1.0, 0.0)
    ).astype(jnp.bfloat16)


def place_keys(start, length, cache_ref, rows_ref, marked, k_scr, v_scr):
    span = cache_ref.shape[0]
    own = rows_ref.shape[0]
    keys = k_scr.shape[2]
    width = KEY_VALUE_HEADS * HEAD_SIZE

    location = lane_index((1, keys))
    place = start + location
    hit = jnp.max(
        jnp.where(marked == place.astype(jnp.float32), 1.0, 0.0), axis=0, keepdims=True
    )
    in_cache = (place < length) & (hit == 0.0) & (location < span)
    usable = in_cache | ((location >= span) & (location < span + own))
    bias = jnp.where(usable, 0.0, NEVER)
    row = lax.broadcasted_iota(jnp.int32, (HEAD_SIZE, keys), 0)
    bias_rows = jnp.where(row == 0, bias, 0.0).astype(jnp.bfloat16)
    pad = keys - span - own
    for slab in range(KEY_VALUE_HEADS // 2):
        columns = slice(slab * LANES, (slab + 1) * LANES)
        value_columns = slice(width + slab * LANES, width + (slab + 1) * LANES)
        tail = [rows_ref[:, columns]]
        value_tail = [rows_ref[:, value_columns]]
        if pad:
            tail.append(jnp.zeros((pad, LANES), jnp.bfloat16))
            value_tail.append(jnp.zeros((pad, LANES), jnp.bfloat16))
        slab_keys = jnp.concatenate([cache_ref[:, columns]] + tail, axis=0).T
        slab_values = jnp.concatenate([cache_ref[:, value_columns]] + value_tail, axis=0)
        for odd in range(2):
            head = 2 * slab + odd
            k_scr[head, :HEAD_SIZE, :] = slab_keys[odd * HEAD_SIZE : (odd + 1) * HEAD_SIZE, :]
            k_scr[head, HEAD_SIZE:, :] = bias_rows
            v_scr[head] = half_with_one(slab_values, odd)


def place_queries(q_ref, q_scr, first):
    rows = q_ref.shape[0]
    pairs = q_ref.shape[1] // LANES
    joined = pairs // q_scr.shape[0]
    stride = q_scr.shape[1] // (2 * joined)
    for pair in range(pairs):
        slab = q_ref[:, pair * LANES : (pair + 1) * LANES].astype(jnp.float32) * (
            1.0 / math.sqrt(HEAD_SIZE)
        )
        for odd in range(2):
            at = (2 * (pair % joined) + odd) * stride + first
            q_scr[pair // joined, at : at + rows, :] = half_with_one(slab, odd)


def attend(q_scr, k_scr, v_scr, s_scr, joined, store, after_step):
    steps = q_scr.shape[0]
    rows = q_scr.shape[1] // (2 * joined)
    group = steps // KEY_VALUE_HEADS

    def scores(step, slot):
        head = lax.div(step, group)
        s_scr[slot] = jnp.dot(q_scr[step], k_scr[head], preferred_element_type=jnp.float32)

    def finish(step, slot):
        head = lax.div(step, group)
        s = s_scr[slot]
        largest = jnp.max(s, axis=1, keepdims=True)
        p = jnp.exp(s - largest).astype(jnp.bfloat16)
        summed = jnp.dot(p, v_scr[head], preferred_element_type=jnp.float32)
        total = summed[:, HEAD_SIZE : HEAD_SIZE + 1]
        mean = summed / total
        lse = jnp.broadcast_to(largest + jnp.log(total), mean.shape)
        low = lane_index((rows, LANES)) < HEAD_SIZE
        for i in range(joined):
            even = slice(2 * i * rows, (2 * i + 1) * rows)
            odd = slice((2 * i + 1) * rows, (2 * i + 2) * rows)
            store(
                step * joined + i,
                jnp.where(low, mean[even], pltpu.roll(mean[odd], HEAD_SIZE, 1)),
                jnp.where(low, lse[even], lse[odd]),
            )

    scores(0, 0)

    def two_steps(j, unused):
        scores(2 * j + 1, 1)
        finish(2 * j, 0)
        scores(jnp.minimum(2 * j + 2, steps - 1), 0)
        finish(2 * j + 1, 1)
        after_step(j)
        return unused

    lax.fori_loop(0, steps // 2, two_steps, 0)


def attention_kernel(
    start_ref, length_ref, q_ref, cache_ref, rows_ref, marked_ref, out_ref, lse_ref,
    q_scr, k_scr, v_scr, s_scr,
):
    place_keys(
        start_ref[0], length_ref[0], cache_ref, rows_ref,
        marked_ref[...].astype(jnp.float32), k_scr, v_scr,
    )
    place_queries(q_ref, q_scr, 0)

    def store(pair, mean, lse):
        out_ref[pair] = mean.astype(jnp.bfloat16)
        lse_ref[pair] = lse

    attend(q_scr, k_scr, v_scr, s_scr, 1, store, lambda j: None)


def attention(queries, cache, row_key_value, start, length, marked):
    rows, width = queries.shape
    pairs = width // LANES
    keys = -(-(cache.shape[0] + row_key_value.shape[0]) // LANES) * LANES
    vmem = pl.BlockSpec(memory_space=pltpu.VMEM)
    smem = pl.BlockSpec(memory_space=pltpu.SMEM)
    return pl.pallas_call(
        attention_kernel,
        out_shape=(
            jax.ShapeDtypeStruct((pairs, rows, LANES), jnp.bfloat16),
            jax.ShapeDtypeStruct((pairs, rows, LANES), jnp.float32),
        ),
        in_specs=[smem, smem, vmem, vmem, vmem, vmem],
        out_specs=(vmem, vmem),
        scratch_shapes=[
            pltpu.VMEM((pairs, 2 * rows, LANES), jnp.bfloat16),
            pltpu.VMEM((KEY_VALUE_HEADS, LANES, keys), jnp.bfloat16),
            pltpu.VMEM((KEY_VALUE_HEADS, keys, LANES), jnp.bfloat16),
            pltpu.VMEM((2, 2 * rows, keys), jnp.float32),
        ],
        compiler_params=pltpu.CompilerParams(vmem_limit_bytes=40 * 1024 * 1024),
        cost_estimate=pl.CostEstimate(
            flops=4 * rows * width * keys,
            bytes_accessed=2 * cache.size + 8 * rows * width,
            transcendentals=rows * keys * width // HEAD_SIZE,
        ),
        name="attention",
    )(start, length, queries, cache, row_key_value, marked)


def chip_at(place, chips):
    return jnp.where(place < chips // 2, 2 * place, 2 * (chips - 1 - place) + 1)


def place_of(chip, chips):
    return jnp.where(chip % 2 == 0, chip // 2, chips - 1 - chip // 2)


def experts_kernel(
    devices, joined, lengths_ref, q_ref, cache_ref, rows_ref, positions_ref,
    resid_ref, gain_ref, ids_ref, gates_ref, gate_hbm, up_hbm, down_hbm, out_ref,
    q_scr, k_scr, v_scr, s_scr, visitor, own_mean, own_lse, host_mean, host_lse,
    far_mean, far_lse, residual,
    visit_sem, mean_send, mean_recv, lse_send, lse_recv,
    x, o, sibling_sums, ring_sums, hidden, w_gate, w_up, w_down,
    weight_sem, gather_send, gather_recv, share_send, share_recv,
    pair_send, pair_recv, ring_send, ring_recv,
):
    rows, half = q_ref.shape[0], q_ref.shape[0] // 2
    model = out_ref.shape[1]
    ff = w_down.shape[0]
    chips = devices // 2
    hops = chips // 2
    me = lax.axis_index("wide")
    core = me % 2
    place = place_of(me // 2, chips)
    sibling = me + 1 - 2 * core
    right = 2 * chip_at((place + 1) % chips, chips) + core
    left = 2 * chip_at((place + chips - 1) % chips, chips) + core

    def remote(source, target, send, recv, device):
        return pltpu.make_async_remote_copy(
            src_ref=source, dst_ref=target, send_sem=send, recv_sem=recv,
            device_id={"wide": device}, device_id_type=pl.DeviceIdType.MESH,
        )

    parts = (pl.ds(0, model // 2), pl.ds(model // 2, model // 2))
    wide_parts = (pl.ds(0, model // 2), pl.ds(model // 2, x.shape[2] - model // 2))

    loads = [
        pltpu.make_async_copy(source.at[0], target, weight_sem.at[i])
        for i, (source, target) in enumerate(
            ((gate_hbm, w_gate), (up_hbm, w_up), (down_hbm, w_down))
        )
    ]
    for load in loads:
        load.start()
    gates = gates_ref[...].T
    ids = ids_ref[...].astype(jnp.float32).T
    mix = gates / jnp.sum(gates, axis=1, keepdims=True)
    lane = lane_index((rows, x.shape[2] - model)).astype(jnp.float32)
    high = jnp.zeros(lane.shape, jnp.float32)
    low = jnp.zeros(lane.shape, jnp.float32)
    for choice in range(ids.shape[1]):
        expert, amount = ids[:, choice : choice + 1], mix[:, choice : choice + 1]
        high = high + jnp.where(lane == expert, amount, 0.0)
        low = low + jnp.where(lane == expert + devices, amount, 0.0)
    low = low - low.astype(jnp.bfloat16).astype(jnp.float32)
    x[0, :rows, model:] = (high + low).astype(jnp.bfloat16)
    ring_sums[hops - 1, half : rows + half] = jnp.zeros((rows, model), jnp.bfloat16)

    barrier = pltpu.get_barrier_semaphore()
    for neighbour in (left, right, sibling):
        pl.semaphore_signal(
            barrier, inc=1, device_id={"wide": neighbour}, device_id_type=pl.DeviceIdType.MESH
        )
    pl.semaphore_wait(barrier, 3)

    visit = remote(q_ref, visitor, visit_sem.at[0], visit_sem.at[1], sibling)
    visit.start()
    document = me // 2
    marked = positions_ref[pl.ds(document, 1), :].astype(jnp.float32)
    marked = jnp.broadcast_to(marked, (LANES, marked.shape[1])).T[:, :1]
    place_keys(
        core * cache_ref.shape[0], lengths_ref[document], cache_ref, rows_ref, marked,
        k_scr, v_scr,
    )
    place_queries(q_ref, q_scr, 0)
    visit.wait_recv()
    place_queries(visitor, q_scr, rows)

    def store(pair, mean, lse):
        own_mean[pair] = mean[:rows]
        own_lse[pair] = lse[:rows]
        host_mean[pair] = mean[rows:].astype(jnp.bfloat16)
        host_lse[pair] = lse[rows:]

    def returned(j):
        two = pl.ds(2 * joined * j, 2 * joined)
        return (
            remote(host_mean.at[two], far_mean.at[two], mean_send.at[j], mean_recv.at[j], sibling),
            remote(host_lse.at[two], far_lse.at[two], lse_send.at[j], lse_recv.at[j], sibling),
        )

    def send_back(j):
        for copy in returned(j):
            copy.start()

    attend(q_scr, k_scr, v_scr, s_scr, joined, store, send_back)

    pairs = own_mean.shape[0]
    squares = jnp.zeros((rows, LANES), jnp.float32)
    for pair in range(pairs):
        if pair % (2 * joined) == 0:
            for copy in returned(pair // (2 * joined)):
                copy.wait_recv()
        columns = slice(pair * LANES, (pair + 1) * LANES)
        near = own_mean[pair]
        far_part = 1.0 / (1.0 + jnp.exp(own_lse[pair] - far_lse[pair]))
        merged = near + (far_mean[pair].astype(jnp.float32) - near) * far_part
        total = resid_ref[:, columns].astype(jnp.float32) + merged.astype(jnp.bfloat16).astype(
            jnp.float32
        )
        residual[:, columns] = total
        squares = squares + total * total
    mean_square = jnp.sum(squares, axis=1, keepdims=True) / model
    x[0, :rows, :model] = (
        residual[...] * lax.rsqrt(mean_square + 1e-06) * gain_ref[...]
    ).astype(jnp.bfloat16)

    def gather(hop, part):
        if isinstance(hop, int) and hop == hops:
            top, bottom = pl.ds(0, half), pl.ds(half, half)
            from_left, from_right = top, bottom if hop == 1 else pl.ds(rows + half, half)
        else:
            top = bottom = None
            from_left, from_right = pl.ds(0, rows), pl.ds(rows, rows)
            if isinstance(hop, int) and hop == 1:
                from_right = pl.ds(0, rows)
        to_left = pl.ds(0, rows) if top is None else top
        to_right = pl.ds(rows, rows) if bottom is None else bottom
        columns = wide_parts[part]
        return (
            remote(x.at[hop - 1, from_left, columns], x.at[hop, to_left, columns],
                   gather_send.at[0, part, hop], gather_recv.at[0, part, hop], right),
            remote(x.at[hop - 1, from_right, columns], x.at[hop, to_right, columns],
                   gather_send.at[1, part, hop], gather_recv.at[1, part, hop], left),
        )

    def share(hop, count, part):
        return remote(x.at[hop, pl.ds(0, count), wide_parts[part]],
                      x.at[hop, pl.ds(count, count), wide_parts[part]],
                      share_send.at[part, hop], share_recv.at[part, hop], sibling)

    def pair(hop, count, part):
        return remote(o.at[hop, pl.ds(count, count), parts[part]],
                      sibling_sums.at[hop, pl.ds(0, count), parts[part]],
                      pair_send.at[part, hop], pair_recv.at[part, hop], sibling)

    def ring(hop, part):
        if isinstance(hop, int) and hop == hops:
            go_left = land_left = pl.ds(0, half)
            go_right, land_right = pl.ds(half, half), pl.ds(rows + half, half)
        else:
            go_left = land_left = pl.ds(0, rows)
            go_right = land_right = pl.ds(rows, rows)
        columns = parts[part]
        return (
            remote(o.at[hop, go_left, columns], ring_sums.at[hop - 1, land_left, columns],
                   ring_send.at[0, part, hop], ring_recv.at[0, part, hop], left),
            remote(o.at[hop, go_right, columns], ring_sums.at[hop - 1, land_right, columns],
                   ring_send.at[1, part, hop], ring_recv.at[1, part, hop], right),
        )

    def chunk_of(size):
        return next(c for c in (256, 128, size) if size % c == 0)

    def run_experts(hop, count):
        tail = x[hop, :count, model:].astype(jnp.float32)
        lane = lane_index(tail.shape)
        weight = jnp.sum(
            jnp.where((lane == me) | (lane == devices + me), tail, 0.0), axis=1, keepdims=True
        )
        step = chunk_of(ff)

        def hide(i, unused):
            columns = pl.ds(pl.multiple_of(i * step, step), step)
            rows_in = x[hop, :count, :model]
            g = jnp.dot(rows_in, w_gate[:, columns], preferred_element_type=jnp.float32)
            u = jnp.dot(rows_in, w_up[:, columns], preferred_element_type=jnp.float32)
            hidden[:count, columns] = (g / (1.0 + jnp.exp(-g)) * u).astype(jnp.bfloat16)
            return unused

        lax.fori_loop(0, ff // step, hide, 0, unroll=True)
        wide = chunk_of(model // 2)

        for part in range(2):

            def expand(i, unused):
                first_column = part * (model // 2) + i * wide
                columns = pl.ds(pl.multiple_of(first_column, wide), wide)
                y = jnp.dot(
                    hidden[:count], w_down[:, columns], preferred_element_type=jnp.float32
                )
                o[hop, :count, columns] = (y * weight).astype(jnp.bfloat16)
                return unused

            lax.fori_loop(0, model // 2 // wide, expand, 0, unroll=True)
            pair(hop, count // 2, part).start()

    def arrive(hop, count, onward):
        for part in range(2):
            coming = gather(hop, part)
            going = (None, None) if onward is None else gather(onward, part)
            for come, go in zip(coming, going):
                come.wait_recv()
                if go is not None:
                    go.start()
            share(hop, count, part).start()
        for part in range(2):
            share(hop, count, part).wait_recv()
        run_experts(hop, 2 * count)

    for part in range(2):
        for copy in gather(1, part):
            copy.start()
    for part in range(2):
        share(0, rows, part).start()
    for load in loads:
        load.wait()
    for part in range(2):
        share(0, rows, part).wait_recv()
    run_experts(0, 2 * rows)

    def middle(hop, unused):
        arrive(hop, 2 * rows, hop + 1)
        return unused

    lax.fori_loop(1, hops - 1, middle, 0)
    if hops > 1:
        arrive(hops - 1, 2 * rows, hops)
    arrive(hops, rows, None)

    def wider(ref, hop, some, columns):
        return ref[hop, some, columns].astype(jnp.float32)

    for part, columns in enumerate(parts):
        pair(hops, rows, part).wait_recv()
        some = pl.ds(0, rows)
        o[hops, some, columns] = (
            wider(o, hops, some, columns) + wider(sibling_sums, hops, some, columns)
        ).astype(jnp.bfloat16)
        for copy in ring(hops, part):
            copy.start()

    def add_up(hop):
        further = hops if isinstance(hop, int) and hop == hops - 1 else hop + 1
        for part, columns in enumerate(parts):
            pair(hop, 2 * rows, part).wait_recv()
            for side, (come, go) in enumerate(zip(ring(further, part), ring(hop, part))):
                come.wait_recv()
                some = pl.ds(side * rows, rows)
                o[hop, some, columns] = (
                    wider(o, hop, some, columns)
                    + wider(sibling_sums, hop, some, columns)
                    + wider(ring_sums, hop, some, columns)
                ).astype(jnp.bfloat16)
                go.start()

    if hops > 1:
        add_up(hops - 1)

    def nearer(i, unused):
        add_up(hops - 2 - i)
        return unused

    lax.fori_loop(0, hops - 2, nearer, 0)
    for part, columns in enumerate(parts):
        pair(0, rows, part).wait_recv()
        for copy in ring(1, part):
            copy.wait_recv()
        some, rest = pl.ds(0, rows), pl.ds(rows, rows)
        out_ref[:, columns] = (
            residual[:, columns]
            + wider(o, 0, some, columns)
            + wider(sibling_sums, 0, some, columns)
            + wider(ring_sums, 0, some, columns)
            + wider(ring_sums, 0, rest, columns)
        ).astype(out_ref.dtype)

    def sent(hop, count):
        for part in range(2):
            for copy in gather(hop, part) + ring(hop, part):
                copy.wait_send()
            share(hop, count, part).wait_send()
            pair(hop, count, part).wait_send()

    visit.wait_send()

    def drained(j, unused):
        for copy in returned(j):
            copy.wait_send()
        return unused

    lax.fori_loop(0, pairs // (2 * joined), drained, 0)
    for part in range(2):
        share(0, rows, part).wait_send()
        pair(0, rows, part).wait_send()
    if hops > 1:
        sent(1, 2 * rows)

    def drain(hop, unused):
        sent(hop, 2 * rows)
        return unused

    lax.fori_loop(2, hops, drain, 0)
    sent(hops, rows)


def scratch_of(rows, wide, model, ff, devices):
    hops = devices // 4
    return [
        ((hops + 1, 4 * rows, wide), jnp.bfloat16),
        ((hops + 1, 4 * rows, model), jnp.bfloat16),
        ((hops + 1, 2 * rows, model), jnp.bfloat16),
        ((hops, 2 * rows, model), jnp.bfloat16),
        ((4 * rows, ff), jnp.bfloat16),
        ((model, ff), jnp.bfloat16),
        ((model, ff), jnp.bfloat16),
        ((ff, model), jnp.bfloat16),
    ]


def fits(buffers):
    return sum(2 * math.prod(shape) for shape, unused in buffers) < 32 * 1024 * 1024


def share_width(devices):
    return -(-2 * devices // LANES) * LANES


def whole_layer(
    lengths, queries, cache, row_key_value, positions, resid, gain, ids, gates,
    w_gate, w_up, w_down, devices,
):
    rows = queries.shape[0]
    model, ff = w_gate.shape[1:]
    wide = model + share_width(devices)
    hops = devices // 4
    pairs = queries.shape[1] // LANES
    keys = -(-(cache.shape[0] + rows) // LANES) * LANES
    anywhere = pl.BlockSpec(memory_space=pl.ANY)
    vmem = pl.BlockSpec(memory_space=pltpu.VMEM)
    smem = pl.BlockSpec(memory_space=pltpu.SMEM)
    dma = pltpu.SemaphoreType.DMA
    half_doc = (pairs, rows, LANES)
    joined = 2 if pairs % (4 * KEY_VALUE_HEADS) == 0 else 1
    return pl.pallas_call(
        functools.partial(experts_kernel, devices, joined),
        out_shape=jax.ShapeDtypeStruct((rows, model), jnp.bfloat16),
        in_specs=[smem] + [vmem] * 8 + [anywhere] * 3,
        out_specs=vmem,
        scratch_shapes=[
            pltpu.VMEM((pairs // joined, 4 * joined * rows, LANES), jnp.bfloat16),
            pltpu.VMEM((KEY_VALUE_HEADS, LANES, keys), jnp.bfloat16),
            pltpu.VMEM((KEY_VALUE_HEADS, keys, LANES), jnp.bfloat16),
            pltpu.VMEM((2, 4 * joined * rows, keys), jnp.float32),
            pltpu.VMEM((rows, queries.shape[1]), jnp.bfloat16),
            pltpu.VMEM(half_doc, jnp.float32),
            pltpu.VMEM(half_doc, jnp.float32),
            pltpu.VMEM(half_doc, jnp.bfloat16),
            pltpu.VMEM(half_doc, jnp.float32),
            pltpu.VMEM(half_doc, jnp.bfloat16),
            pltpu.VMEM(half_doc, jnp.float32),
            pltpu.VMEM((rows, model), jnp.float32),
            dma((2,)),
        ]
        + [dma((pairs // (2 * joined),))] * 4
        + [
            pltpu.VMEM(shape, kind)
            for shape, kind in scratch_of(rows, wide, model, ff, devices)
        ]
        + [dma((3,))]
        + [dma((2, 2, hops + 1)), dma((2, 2, hops + 1)), dma((2, hops + 1)), dma((2, hops + 1))]
        + [dma((2, hops + 1)), dma((2, hops + 1)), dma((2, 2, hops + 1)), dma((2, 2, hops + 1))],
        compiler_params=pltpu.CompilerParams(
            collective_id=0, has_side_effects=True, vmem_limit_bytes=58 * 1024 * 1024
        ),
        cost_estimate=pl.CostEstimate(
            flops=6 * rows * devices * model * ff + 8 * rows * model * keys,
            bytes_accessed=6 * model * ff + 2 * cache.size,
            transcendentals=rows * devices * ff,
        ),
        name="whole_layer",
    )(
        lengths, queries, cache, row_key_value, positions, resid, gain, ids, gates,
        w_gate, w_up, w_down,
    )


def local(
    query_rows,
    row_key_value,
    key_value_cache,
    resid,
    norm_gain,
    lengths,
    positions,
    expert_ids,
    gate_scores,
    w_gate,
    w_up,
    w_down,
):
    rows = query_rows.shape[0]
    width = query_rows.shape[1]
    span = key_value_cache.shape[0]
    device = lax.axis_index("wide")
    experts = lax.axis_size("wide")
    doc_index = device // 2
    half_index = device % 2

    model, ff = w_gate.shape[1:]
    buffers = scratch_of(rows, model + share_width(experts), model, ff, experts)
    if experts % 4 == 0 and fits(buffers):
        return whole_layer(
            lengths, query_rows, key_value_cache, row_key_value, positions, resid,
            norm_gain[None, :], expert_ids.T, gate_scores.T, w_gate, w_up, w_down, experts,
        )

    mix = gate_scores / jnp.sum(gate_scores, axis=-1, keepdims=True)
    chosen = expert_ids[..., None] == jnp.arange(experts, dtype=jnp.int32)
    share = jnp.sum(jnp.where(chosen, mix[..., None], 0.0), axis=1)
    high = share.astype(jnp.bfloat16)
    low = (share - high.astype(jnp.float32)).astype(jnp.bfloat16)
    spare = -(2 * experts) % LANES
    shares = jnp.concatenate([high, low, jnp.zeros((rows, spare), jnp.bfloat16)], axis=1)

    length = lax.dynamic_slice_in_dim(lengths, doc_index, 1, 0)
    marked = lax.dynamic_index_in_dim(positions, doc_index, 0, keepdims=False)[:, None]
    start = jnp.reshape(half_index * span, (1,)).astype(jnp.int32)
    visitor = swapped(query_rows, "wide", 0)
    means, lse = attention(
        jnp.concatenate([query_rows, visitor], axis=0),
        key_value_cache, row_key_value, start, length, marked,
    )
    far_mean = swapped(means[:, rows:], "wide", 0).astype(jnp.float32)
    far_lse = swapped(lse[:, rows:], "wide", 0)
    own_mean = means[:, :rows].astype(jnp.float32)
    own_lse = lse[:, :rows]
    far_part = 1.0 / (1.0 + jnp.exp(own_lse - far_lse))
    merged = own_mean + (far_mean - own_mean) * far_part
    attended = jnp.swapaxes(merged, 0, 1).reshape(rows, width).astype(jnp.bfloat16)

    residual = resid.astype(jnp.float32) + attended.astype(jnp.float32)
    normed = (
        residual
        * lax.rsqrt(jnp.mean(residual * residual, axis=-1, keepdims=True) + 1e-06)
        * norm_gain
    ).astype(jnp.bfloat16)

    first = jnp.concatenate([normed, shares], axis=1)

    gathered = lax.all_gather(first, "wide", axis=0, tiled=True)
    everyone = gathered[:, :model]
    weight = sum(
        lax.dynamic_slice_in_dim(gathered, model + device + part * experts, 1, 1).astype(
            jnp.float32
        )
        for part in range(2)
    )
    gate_act = jnp.dot(everyone, w_gate[0], preferred_element_type=jnp.float32)
    up_act = jnp.dot(everyone, w_up[0], preferred_element_type=jnp.float32)
    hidden = (jax.nn.silu(gate_act) * up_act).astype(jnp.bfloat16)
    expert_out = jnp.dot(hidden, w_down[0], preferred_element_type=jnp.float32)
    weighted = (expert_out * weight).astype(jnp.bfloat16)
    routed = lax.psum_scatter(weighted, "wide", scatter_dimension=0, tiled=True)
    return (residual + routed.astype(jnp.float32)).astype(jnp.bfloat16)


def solution(mesh):
    return jax.shard_map(
        local,
        mesh=mesh,
        in_specs=(
            P(("grp", "wide"), None),
            P(("grp", "wide"), None),
            P(("grp", "wide"), None),
            P(("grp", "wide"), None),
            P(),
            P("grp"),
            P("grp", None),
            P(("grp", "wide"), None),
            P(("grp", "wide"), None),
            P("wide", None, None),
            P("wide", None, None),
            P("wide", None, None),
        ),
        out_specs=P(("grp", "wide"), None),
        check_vma=False,
    )
```
